256 devices in a mesh: seq: 2 (over core), row: 32 (over z, x), col: 4 (over y).
Axes of the slice: x: 4, y: 4, z: 8, core: 2. Of those that a mesh axis runs over, the one named last changes fastest.
Arguments:
- tokens: bfloat16 [8192, 8192], P(('seq', 'row'), 'col'), as said below
- positions: int32 [8192], replicated, may hold values from 0 to 6143, as said below
- w_query: bfloat16 [8192, 8192], P('row', 'col'), as said below
- w_key: bfloat16 [8192, 1024], P(None, 'col'), as said below
- w_value: bfloat16 [8192, 1024], P(None, 'col'), may hold values from -0.125 to 0.125
Outputs:
- context: bfloat16 [8192, 8192], P(('seq', 'row'), 'col')
The draws below stay inside these ranges and needn't reach their ends.
Inputs may be any that keep to these rules, and one draw needn't show every extreme that they name: positions[i] is 0 at a document's first token and positions[i - 1] + 1 otherwise; the sequence holds at most four documents. `tokens`: real-valued hidden states of order one. `w_query`: real-valued weights. `w_key`: real-valued weights.
All inputs are finite; a program needn't handle non-finite values.
Results may differ from the reference program's by a relative error of at most 0.0085.
Values may be sent and summed in bfloat16 or wider, within the bound.
A program may use at most 128 MiB of HBM per device.

```python
import math
import jax
import jax.numpy as jnp
from jax import lax

D = 8192
HEADS = 64
KVH = 8
HD = 128
KW = 1024
LENGTH = 8192


def draw_w_query(key, part):
    key = jax.random.fold_in(key, 1)
    matrix = jax.random.truncated_normal(key, -4.0, 4.0, (D, HEADS * HD), jnp.float32) * (2.0 / math.sqrt(D))
    return matrix.astype(jnp.bfloat16)


def draw_w_key(key, part):
    key = jax.random.fold_in(key, 2)
    matrix = jax.random.truncated_normal(key, -4.0, 4.0, (D, KVH * HD), jnp.float32) * (1.0 / math.sqrt(D))
    return matrix.astype(jnp.bfloat16)


def draw_tokens(key, part):
    key = jax.random.fold_in(key, 3)
    values = jax.random.truncated_normal(key, -6.0, 6.0, (LENGTH, D), jnp.float32)
    return values.astype(jnp.bfloat16)


def draw_positions(key, part):
    key = jax.random.fold_in(key, 4)
    later = jax.random.randint(key, (2,), 3 * LENGTH // 4, LENGTH, dtype=jnp.int32)
    boundaries = jnp.concatenate([jnp.full((1,), 3 * LENGTH // 4, jnp.int32), later]).astype(jnp.int32)
    token_index = jnp.arange(LENGTH, dtype=jnp.int32)
    begins = jnp.where(boundaries[:, None] <= token_index[None, :], boundaries[:, None], 0)
    return (token_index - jnp.max(begins, axis=0)).astype(jnp.int32)


def steps_of(key, extent, pieces, smallest, largest):
    def one(dim, parts):
        draws = jax.random.uniform(jax.random.fold_in(jax.random.fold_in(key, 6), dim), (parts,), jnp.float32, smallest / len(pieces), largest / len(pieces))
        return jnp.repeat(jnp.exp(draws), extent[dim] // parts).reshape((-1,) + (1,) * (len(extent) - dim - 1))

    level = one(*pieces[0])
    for cut in pieces[1:]:
        level = level * one(*cut)
    return level


def bell_draw(own_key, extent, width, limit, pieces=(), kind=jnp.bfloat16):
    loudness = steps_of(own_key, extent, pieces, -0.22, 0.18) if pieces else 1.0
    result = jax.random.normal(own_key, extent, jnp.float32) * width * loudness
    return jnp.minimum(jnp.maximum(result, -limit), limit).astype(kind)


def setup_inputs(seed: int = 0) -> dict:
    splits = jax.random.split(jax.random.key(seed), 6)
    tokens = draw_tokens(jax.random.fold_in(splits[5], 71), 0)
    positions = draw_positions(jax.random.fold_in(splits[5], 71), 0)
    w_query = draw_w_query(jax.random.fold_in(splits[5], 71), 0)
    w_key = draw_w_key(jax.random.fold_in(splits[5], 71), 0)
    w_value = bell_draw(splits[4], (D, KW), (D // 4) ** -0.5, 0.125, ((1, 4),))
    return {"tokens": tokens, "positions": positions, "w_query": w_query, "w_key": w_key, "w_value": w_value}


def reference(tokens, positions, w_query, w_key, w_value):
    length = tokens.shape[0]
    group_size = HEADS // KVH
    query = jnp.dot(tokens, w_query, preferred_element_type=jnp.float32).astype(jnp.bfloat16)
    key_rows = jnp.dot(tokens, w_key, preferred_element_type=jnp.float32).astype(jnp.bfloat16)
    value_rows = jnp.dot(tokens, w_value, preferred_element_type=jnp.float32).astype(jnp.bfloat16)
    query_four = query.reshape(length, KVH, group_size, HD).astype(jnp.float32)
    key_three = key_rows.reshape(length, KVH, HD).astype(jnp.float32)
    value_three = value_rows.reshape(length, KVH, HD).astype(jnp.float32)
    token_index = jnp.arange(length, dtype=jnp.int32)
    doc_begin = token_index - positions.astype(jnp.int32)
    block_rows = math.gcd(length, 256)
    score_scale = 1.0 / math.sqrt(HD)

    def one_block(number):
        first_row = (number * block_rows).astype(jnp.int32)
        query_block = lax.dynamic_slice_in_dim(query_four, first_row, block_rows, 0)
        query_index = first_row + jnp.arange(block_rows, dtype=jnp.int32)
        doc_start = lax.dynamic_slice_in_dim(doc_begin, first_row, block_rows, 0)
        scores = jnp.einsum('qhgd,khd->hgqk', query_block, key_three) * score_scale
        allowed = (token_index[None, :] <= query_index[:, None]) & (token_index[None, :] >= doc_start[:, None])
        scores = jnp.where(allowed, scores, -1e+30)
        row_max = lax.optimization_barrier(jnp.max(scores, axis=-1, keepdims=True))
        exponent = jnp.where(allowed, jnp.exp(scores - row_max), 0.0)
        denom_sum = lax.optimization_barrier(jnp.sum(exponent, axis=-1))
        rounded = lax.optimization_barrier(exponent.astype(jnp.bfloat16))
        mixed_rows = jnp.einsum('hgqk,khd->qhgd', rounded.astype(jnp.float32), value_three)
        mixed_rows = mixed_rows / jnp.transpose(denom_sum, (2, 0, 1))[..., None]
        return mixed_rows.reshape(block_rows, KVH * group_size * HD).astype(jnp.bfloat16)
    blocks = lax.map(one_block, jnp.arange(length // block_rows, dtype=jnp.int32))
    return blocks.reshape(length, HEADS * HD)
```

```python
import functools
import math

import jax
import jax.numpy as jnp
from jax import lax
from jax.experimental import pallas as pl
from jax.experimental.pallas import tpu as pltpu
from jax.sharding import PartitionSpec as P

HD = 128
NX, NY, NZ = 4, 4, 8
ROWS = 128
CHUNK = NX * ROWS
MESH = pl.DeviceIdType.MESH
LOG2E = 1.4426950408889634
NEG = -1e30


def place():
    row = lax.axis_index("row")
    return lax.axis_index("seq"), row // NX, row % NX, lax.axis_index("col")


def greet(partners):
    barrier = pltpu.get_barrier_semaphore()
    for partner in partners:
        pl.semaphore_signal(barrier, inc=1, device_id=partner, device_id_type=MESH)
    pl.semaphore_wait(barrier, len(partners))


def project_kernel(
    tok_ref, wq_ref, wk_ref, wv_ref, q_ref, kv_ref, tok, wq, wkv, acc, qsend, loc, ssem, rsem
):
    core, z, x, y = place()
    sib = 1 - core

    def at(dz=0, dx=0, dy=0, c=core):
        return (c, (z + dz) % NZ * NX + (x + dx) % NX, (y + dy) % NY)

    step = {"x+": (0, 1, 0), "x-": (0, -1, 0), "y+": (0, 0, 1), "y-": (0, 0, -1),
            "z+": (1, 0, 0), "z-": (-1, 0, 0)}
    slots = {}
    sent = []

    def slot(key):
        return slots.setdefault(key, len(slots))

    def put(key, src, dst, device):
        i = slot(key)
        copy = pltpu.make_async_remote_copy(
            src_ref=src, dst_ref=dst, send_sem=ssem.at[i], recv_sem=rsem.at[i],
            device_id=device, device_id_type=MESH)
        copy.start()
        sent.append(copy)

    def take(key, dst):
        i = slot(key)
        pltpu.make_async_remote_copy(
            src_ref=dst, dst_ref=dst, send_sem=ssem.at[i], recv_sem=rsem.at[i],
            device_id=at(c=sib), device_id_type=MESH).wait_recv()

    head = x // 2
    my_w = pl.ds(pl.multiple_of(x * 512 + core * 256, 256), 256)
    head_cols = pl.ds(pl.multiple_of(head * HD, HD), HD)
    loads = [
        pltpu.make_async_copy(tok_ref, tok.at[x, y], loc.at[0]),
        pltpu.make_async_copy(wq_ref.at[:, my_w], wq.at[core, z * NX + x], loc.at[1]),
        pltpu.make_async_copy(wk_ref.at[:, head_cols], wkv.at[:, pl.ds(0, HD)], loc.at[2]),
        pltpu.make_async_copy(wv_ref.at[:, head_cols], wkv.at[:, pl.ds(HD, HD)], loc.at[3]),
    ]
    for load in loads:
        load.start()

    greet([at(dx=1), at(dx=2), at(dx=3), at(dy=1), at(dy=3), at(dz=1), at(dz=7), at(c=sib)])

    for dx in (1, 3, 2):
        cols = pl.ds(pl.multiple_of((x + dx) % NX * 512 + core * 256, 256), 256)
        put(("w", dx), wq_ref.at[:, cols], wq.at[core, z * NX + x], at(dx=dx))

    def block(u, v, h, q):
        start, size = (h * 64, 64) if q is None else (h * 64 + q * 32, 32)
        return tok.at[(x + u) % NX, (y + v) % NY, pl.ds(start, size)]

    def orient(h, a, b):
        return (a, b) if h == 0 else (b, a)

    def axis(h, order):
        return ("y", "x")[h] if order == 0 else ("x", "y")[h]

    def token_put(h, order, sign, a, b, q=None):
        d = axis(h, order) + sign
        ref = block(*orient(h, a, b), h, q)
        dz, dx, dy = step[d]
        put((d, h, a, b, q), ref, ref, at(dx=dx, dy=dy))

    def token_take(h, order, sign, a, b, q=None):
        d = axis(h, order) + sign
        move = -1 if sign == "+" else 1
        a2, b2 = (a, b + move) if order == 0 else (a + move, b)
        take((d, h, a, b, q), block(*orient(h, a2, b2), h, q))

    loads[0].wait()
    for h in (0, 1):
        for sign in "+-":
            token_put(h, 0, sign, 0, 0)
    for h in (0, 1):
        for sign in "+-":
            token_put(h, 1, sign, 0, 0)

    def ring_step(name, unit, sign, dist, h):
        way = -1 if sign == "+" else 1
        ref = unit(way * dist, h)
        if dist:
            take((name, sign, dist, h), ref)
        if dist < 3 or (dist == 3 and h == (0 if sign == "+" else 1)):
            dz = step["z" + sign][0]
            put((name, sign, dist + 1, h), ref, ref, at(dz=dz))
        if dist or sign == "+":
            put((name, "c", way * dist, h), ref, ref, at(c=sib))

    def w_unit(dz, h):
        return wq.at[core, pl.ds((z + dz) % NZ * NX + 2 * h, 2)]

    loads[1].wait()
    for dx in (1, 3, 2):
        take(("w", dx), wq.at[core, z * NX + (x - dx) % NX])
    for h in (0, 1):
        for sign in "+-":
            ring_step("W", w_unit, sign, 0, h)

    def w_round(dist, h):
        for sign in "+-":
            ring_step("W", w_unit, sign, dist, h)

    for sign, q in (("+", 0), ("-", 1)):
        for h in (0, 1):
            b = -1 if sign == "+" else 1
            token_take(h, 0, sign, 0, 0)
            token_put(h, 0, sign, 0, b, q)
            for sign2 in "+-":
                token_put(h, 1, sign2, 0, b)
    w_round(1, 0)
    for sign, q in (("+", 0), ("-", 1)):
        for h in (0, 1):
            token_take(h, 1, sign, 0, 0)
            token_put(h, 1, sign, -1 if sign == "+" else 1, 0, q)
    w_round(1, 1)
    for sign, q in (("+", 0), ("-", 1)):
        for h in (0, 1):
            b = -1 if sign == "+" else 1
            token_take(h, 0, sign, 0, b, q)
            for sign2 in "+-":
                token_put(h, 1, sign2, 0, 2 * b, q)
    w_round(2, 0)
    for b in (-1, 1):
        for sign, q in (("+", 0), ("-", 1)):
            for h in (0, 1):
                token_take(h, 1, sign, 0, b)
                token_put(h, 1, sign, -1 if sign == "+" else 1, b, q)
        w_round(2, 1) if b == -1 else w_round(3, 0)
    for sign, q in (("+", 0), ("-", 1)):
        for h in (0, 1):
            b = -2 if sign == "+" else 2
            token_take(h, 1, sign, 0, b, q)
            token_put(h, 1, sign, -1 if sign == "+" else 1, b, q)
    for sign, q in (("+", 1), ("-", 0)):
        for h in (0, 1):
            token_take(h, 1, sign, 0, -2 if q == 0 else 2, q)
    w_round(3, 1)
    for sign, q in (("+", 0), ("-", 1)):
        a = -1 if sign == "+" else 1
        for b in (0, -1, 1, 2 * a):
            for h in (0, 1):
                token_take(h, 1, sign, a, b, q)

    def dot(weights, width):
        acc[:, pl.ds(0, width)] = jnp.zeros((CHUNK, width), jnp.float32)

        def body(j, carry):
            col = pl.multiple_of(j % 2 * 1024, 1024)
            left = tok[:, pl.ds(j // 2, 1), :, pl.ds(col, 1024)].reshape(CHUNK, 1024)
            acc[:, pl.ds(0, width)] += jnp.dot(
                left, weights(j), preferred_element_type=jnp.float32)
            return carry

        lax.fori_loop(0, 8, body, 0)

    loads[2].wait()
    loads[3].wait()
    dot(lambda j: wkv[pl.ds(pl.multiple_of(j * 1024, 1024), 1024), :], 2 * HD)
    kv_ref[pl.ds(core, 1), pl.ds(z, 1)] = (
        acc[:, pl.ds(0, 2 * HD)].astype(jnp.bfloat16).reshape(1, 1, CHUNK, 2 * HD))

    def kv_unit(dz, h):
        return kv_ref.at[core, (z + dz) % NZ, pl.ds(h * 256, 256)]

    def kv_round(dist, h):
        for sign in "+-":
            ring_step("K", kv_unit, sign, dist, h)

    kv_round(0, 0)
    kv_round(0, 1)
    ring_step("W", w_unit, "+", 4, 0)
    ring_step("W", w_unit, "-", 4, 1)
    for dz in (0, -1, 1, -2, 2, -3, 3):
        for h in (0, 1):
            take(("W", "c", dz, h), wq.at[sib, pl.ds((z + dz) % NZ * NX + 2 * h, 2)])
    for dz, h in ((-4, 0), (4, 1)):
        take(("W", "c", dz, h), wq.at[sib, pl.ds((z + dz) % NZ * NX + 2 * h, 2)])

    def q_dot(c):
        dot(lambda j: wq[pl.ds(c, 1), pl.ds(j * 4, 4)].reshape(1024, 256), 256)

    q_dot(sib)
    qsend[...] = acc[:, pl.ds(0, 256)].astype(jnp.bfloat16)
    put(("Q",), qsend, q_ref.at[core], at(c=sib))
    kv_round(1, 0)
    kv_round(1, 1)
    q_dot(core)
    q_ref[pl.ds(core, 1)] = acc[:, pl.ds(0, 256)].astype(jnp.bfloat16).reshape(1, CHUNK, 256)
    for dist in (2, 3):
        kv_round(dist, 0)
        kv_round(dist, 1)
    ring_step("K", kv_unit, "+", 4, 0)
    ring_step("K", kv_unit, "-", 4, 1)
    take(("Q",), q_ref.at[sib])
    for dz in (0, -1, 1, -2, 2, -3, 3):
        for h in (0, 1):
            take(("K", "c", dz, h), kv_ref.at[sib, (z + dz) % NZ, pl.ds(h * 256, 256)])
    for dz, h in ((-4, 0), (4, 1)):
        take(("K", "c", dz, h), kv_ref.at[sib, (z + dz) % NZ, pl.ds(h * 256, 256)])
    for copy in sent:
        copy.wait_send()


COPIES = 128


def project(tokens, w_query, w_key, w_value):
    anywhere = pl.BlockSpec(memory_space=pltpu.HBM)
    return pl.pallas_call(
        project_kernel,
        name="project",
        out_shape=[
            jax.ShapeDtypeStruct((2, CHUNK, 256), jnp.bfloat16),
            jax.ShapeDtypeStruct((2, NZ, CHUNK, 2 * HD), jnp.bfloat16),
        ],
        in_specs=[anywhere] * 4,
        out_specs=[pl.BlockSpec(memory_space=pltpu.VMEM)] * 2,
        scratch_shapes=[
            pltpu.VMEM((NX, NY, ROWS, 2048), jnp.bfloat16),
            pltpu.VMEM((2, NZ * NX, 256, 256), jnp.bfloat16),
            pltpu.VMEM((8192, 2 * HD), jnp.bfloat16),
            pltpu.VMEM((CHUNK, 256), jnp.float32),
            pltpu.VMEM((CHUNK, 256), jnp.bfloat16),
            pltpu.SemaphoreType.DMA((4,)),
            pltpu.SemaphoreType.DMA((COPIES,)),
            pltpu.SemaphoreType.DMA((COPIES,)),
        ],
        compiler_params=pltpu.CompilerParams(
            collective_id=0, has_side_effects=True, vmem_limit_bytes=56 * 2**20),
    )(tokens, w_query, w_key, w_value)


QT = 256
KT = 512


def attend_kernel(pos_s, pos_v, q_ref, kv_ref, o_ref, m_sc, l_sc, acc_sc):
    z = lax.axis_index("row") // NX
    scale = LOG2E / math.sqrt(HD)
    for s in range(2):
        for t in range(CHUNK // QT):
            base = s * (NZ * CHUNK) + z * CHUNK + t * QT
            first_doc = base - pos_s[base]
            last_doc = base + QT - 1 - pos_s[base + QT - 1]
            diag = s * NZ + z
            queries = jnp.concatenate(
                [q_ref[s, t * QT:(t + 1) * QT, :HD], q_ref[s, t * QT:(t + 1) * QT, HD:]], axis=0)
            m_sc[...] = jnp.full_like(m_sc, NEG)
            l_sc[...] = jnp.zeros_like(l_sc)
            acc_sc[...] = jnp.zeros_like(acc_sc)

            def block(kb, masked):
                keys = kv_ref[pl.ds(kb, 1), :, :HD].reshape(KT, HD)
                values = kv_ref[pl.ds(kb, 1), :, HD:].reshape(KT, HD)
                scores = lax.dot_general(
                    queries, keys, (((1,), (1,)), ((), ())), preferred_element_type=jnp.float32)
                if masked:
                    starts = []
                    for r in range(QT // 128):
                        at_row = base // 128 + r
                        pos = pos_v[pl.ds(at_row, 1), :]
                        lane = lax.broadcasted_iota(jnp.int32, (1, 128), 1)
                        begin = at_row * 128 + lane - pos
                        starts.append(jnp.broadcast_to(begin, (128, 128)).T)
                    begin = jnp.concatenate(starts, axis=0)
                    begin = jnp.concatenate([begin] * (KT // 128), axis=1)
                    row = base + lax.broadcasted_iota(jnp.int32, (QT, KT), 0)
                    key = kb * KT + lax.broadcasted_iota(jnp.int32, (QT, KT), 1)
                    allowed = (key <= row) & (key >= begin)
                    allowed = jnp.concatenate([allowed, allowed], axis=0)
                    scores = jnp.where(allowed, scores, NEG)
                old_max = m_sc[...]
                new_max = jnp.maximum(old_max, jnp.max(scores, axis=1, keepdims=True))
                wide_max = jnp.concatenate([new_max] * (KT // 128), axis=1)
                exponent = jnp.exp2((scores - wide_max) * scale)
                if masked:
                    exponent = jnp.where(allowed, exponent, 0.0)
                shrink = jnp.exp2((old_max - new_max) * scale)
                m_sc[...] = new_max
                l_sc[...] = l_sc[...] * shrink + jnp.sum(exponent, axis=1, keepdims=True)
                acc_sc[...] = acc_sc[...] * shrink + jnp.dot(
                    exponent.astype(jnp.bfloat16), values, preferred_element_type=jnp.float32)

            low = first_doc // KT

            def body(kb, carry):
                whole = kb * KT >= last_doc

                @pl.when(whole)
                def _():
                    block(kb, False)

                @pl.when(jnp.logical_not(whole))
                def _():
                    block(kb, True)

                return carry

            lax.fori_loop(low, diag, body, 0)
            block(diag, True)
            result = (acc_sc[...] / l_sc[...]).astype(jnp.bfloat16)
            o_ref[s, t * QT:(t + 1) * QT, :HD] = result[:QT]
            o_ref[s, t * QT:(t + 1) * QT, HD:] = result[QT:]


def attend(positions, q, kv):
    vmem = pl.BlockSpec(memory_space=pltpu.VMEM)
    return pl.pallas_call(
        attend_kernel,
        name="attend",
        out_shape=jax.ShapeDtypeStruct((2, CHUNK, 256), jnp.bfloat16),
        in_specs=[pl.BlockSpec(memory_space=pltpu.SMEM), vmem, vmem, vmem],
        out_specs=vmem,
        scratch_shapes=[
            pltpu.VMEM((2 * QT, 128), jnp.float32),
            pltpu.VMEM((2 * QT, 128), jnp.float32),
            pltpu.VMEM((2 * QT, HD), jnp.float32),
        ],
        compiler_params=pltpu.CompilerParams(vmem_limit_bytes=56 * 2**20),
    )(positions, positions.reshape(64, 128), q, kv.reshape(2 * NZ, CHUNK, 2 * HD))


def spread_kernel(ctx_ref, out_ref, loc, ssem, rsem):
    core, z, x, y = place()
    moves = [(dc, dx) for dx in (2, 1, 3, 0) for dc in (1, 0)][:-1]

    def at(dc, dx):
        return ((core + dc) % 2, z * NX + (x + dx) % NX, y)

    def cols(c, xx):
        return pl.ds(pl.multiple_of(xx * 512 + c * 256, 256), 256)

    def piece(c, xx):
        return ctx_ref.at[c, pl.ds(pl.multiple_of(xx * ROWS, ROWS), ROWS)]

    greet([at(dc, dx) for dc, dx in moves])
    copies = []
    for i, (dc, dx) in enumerate(moves):
        copy = pltpu.make_async_remote_copy(
            src_ref=piece((core + dc) % 2, (x + dx) % NX), dst_ref=out_ref.at[:, cols(core, x)],
            send_sem=ssem.at[i], recv_sem=rsem.at[i], device_id=at(dc, dx), device_id_type=MESH)
        copy.start()
        copies.append(copy)
    own = pltpu.make_async_copy(piece(core, x), out_ref.at[:, cols(core, x)], loc)
    own.start()
    own.wait()
    for copy in copies:
        copy.wait_send()
    for i, (dc, dx) in enumerate(moves):
        land = out_ref.at[:, cols((core + dc) % 2, (x - dx) % NX)]
        pltpu.make_async_remote_copy(
            src_ref=land, dst_ref=land, send_sem=ssem.at[i], recv_sem=rsem.at[i],
            device_id=at(dc, dx), device_id_type=MESH).wait_recv()


def spread(ctx):
    vmem = pl.BlockSpec(memory_space=pltpu.VMEM)
    return pl.pallas_call(
        spread_kernel,
        name="spread",
        out_shape=jax.ShapeDtypeStruct((ROWS, 2048), jnp.bfloat16),
        in_specs=[vmem],
        out_specs=vmem,
        scratch_shapes=[
            pltpu.SemaphoreType.DMA,
            pltpu.SemaphoreType.DMA((7,)),
            pltpu.SemaphoreType.DMA((7,)),
        ],
        compiler_params=pltpu.CompilerParams(collective_id=1, has_side_effects=True),
    )(ctx)


def local(tokens, positions, w_query, w_key, w_value):
    q, kv = project(tokens, w_query, w_key, w_value)
    return spread(attend(positions, q, kv))


def solution(mesh):
    in_specs = (P(("seq", "row"), "col"), P(), P("row", "col"), P(None, "col"), P(None, "col"))
    out_specs = P(("seq", "row"), "col")
    return jax.shard_map(local, mesh=mesh, in_specs=in_specs, out_specs=out_specs, check_vma=False)
```

```python
import functools
import math

import jax
import jax.numpy as jnp
from jax import lax
from jax.experimental import pallas as pl
from jax.experimental.pallas import tpu as pltpu
from jax.sharding import PartitionSpec as P

HD = 128
NX, NY, NZ = 4, 4, 8
ROWS = 128
CHUNK = NX * ROWS
MESH = pl.DeviceIdType.MESH
LOG2E = 1.4426950408889634
NEG = -1e30


def place():
    row = lax.axis_index("row")
    return lax.axis_index("seq"), row // NX, row % NX, lax.axis_index("col")


def greet(partners):
    barrier = pltpu.get_barrier_semaphore()
    for partner in partners:
        pl.semaphore_signal(barrier, inc=1, device_id=partner, device_id_type=MESH)
    pl.semaphore_wait(barrier, len(partners))


def kernel_body(
    tok_ref, pos_ref, wq_ref, wk_ref, wv_ref, out_ref, tok, wq, wkv, kv, feat, q, qsend, qland, acc,
    docs, top, ctx_acc, ctx, loc, ssem, rsem, ksend, krecv,
    osend, orecv
):
    core, z, x, y = place()
    sib = 1 - core

    def at(dz=0, dx=0, dy=0, c=core):
        return (c, (z + dz) % NZ * NX + (x + dx) % NX, (y + dy) % NY)

    step = {"x+": (0, 1, 0), "x-": (0, -1, 0), "y+": (0, 0, 1), "y-": (0, 0, -1),
            "z+": (1, 0, 0), "z-": (-1, 0, 0)}
    slots = {}
    sent = []

    def slot(key):
        return slots.setdefault(key, len(slots))

    def put(key, src, dst, device):
        i = slot(key)
        copy = pltpu.make_async_remote_copy(
            src_ref=src, dst_ref=dst, send_sem=ssem.at[i], recv_sem=rsem.at[i],
            device_id=device, device_id_type=MESH)
        copy.start()
        sent.append(copy)

    def take(key, dst):
        i = slot(key)
        pltpu.make_async_remote_copy(
            src_ref=dst, dst_ref=dst, send_sem=ssem.at[i], recv_sem=rsem.at[i],
            device_id=at(c=sib), device_id_type=MESH).wait_recv()

    def document_features():
        first = (pos_ref[...] == 0).astype(jnp.bfloat16)
        r = lax.broadcasted_iota(jnp.int32, (HD, HD), 0)
        c = lax.broadcasted_iota(jnp.int32, (HD, HD), 1)
        within = jnp.dot(first, (r <= c).astype(jnp.bfloat16), preferred_element_type=jnp.float32)
        total = jnp.broadcast_to(within[:, HD - 1:], within.shape).astype(jnp.bfloat16)
        before = (c < r).astype(jnp.bfloat16)[:64, :64]
        docs[...] = within + jnp.dot(before, total, preferred_element_type=jnp.float32)

        def body(b, carry):
            for part in range(CHUNK // HD):
                row = docs[pl.ds(b * (CHUNK // HD) + part, 1), :]
                hot = jnp.broadcast_to(row, (HD, HD)) == r.astype(jnp.float32)
                feat[pl.ds(b, 1), part * HD:(part + 1) * HD, :] = (
                    hot.astype(jnp.float32).T.astype(jnp.bfloat16).reshape(1, HD, HD))
            return carry

        lax.fori_loop(0, 2 * NZ, body, 0)
        for s in range(2):
            hot = feat[pl.ds(s * NZ + z, 1)].reshape(CHUNK, HD).astype(jnp.float32)
            bar = ((1.0 - hot) * NEG).astype(jnp.bfloat16)
            for g in range(2):
                q[s, g, :, HD:] = bar

    head = x // 2
    my_w = pl.ds(pl.multiple_of(x * 512 + core * 256, 256), 256)
    head_cols = pl.ds(pl.multiple_of(head * HD, HD), HD)
    loads = [
        pltpu.make_async_copy(tok_ref, tok.at[x, y], loc.at[0]),
        pltpu.make_async_copy(wq_ref.at[:, my_w], wq.at[core, z * NX + x], loc.at[1]),
        pltpu.make_async_copy(wk_ref.at[:, head_cols], wkv.at[:, pl.ds(0, HD)], loc.at[2]),
        pltpu.make_async_copy(wv_ref.at[:, head_cols], wkv.at[:, pl.ds(HD, HD)], loc.at[3]),
    ]
    for load in loads:
        load.start()

    greet([at(dx=1), at(dx=2), at(dx=3), at(dy=1), at(dy=3), at(dz=1), at(dz=7), at(c=sib),
           at(dx=1, c=sib), at(dx=2, c=sib), at(dx=3, c=sib)])

    for dx in (1, 3, 2):
        cols = pl.ds(pl.multiple_of((x + dx) % NX * 512 + core * 256, 256), 256)
        put(("w", dx), wq_ref.at[:, cols], wq.at[core, z * NX + x], at(dx=dx))

    def block(u, v, h, q):
        start, size = (h * 64, 64) if q is None else (h * 64 + q * 32, 32)
        return tok.at[(x + u) % NX, (y + v) % NY, pl.ds(start, size)]

    def orient(h, a, b):
        return (a, b) if h == 0 else (b, a)

    def axis(h, order):
        return ("y", "x")[h] if order == 0 else ("x", "y")[h]

    def token_put(h, order, sign, a, b, q=None):
        d = axis(h, order) + sign
        ref = block(*orient(h, a, b), h, q)
        dz, dx, dy = step[d]
        put((d, h, a, b, q), ref, ref, at(dx=dx, dy=dy))

    def token_take(h, order, sign, a, b, q=None):
        d = axis(h, order) + sign
        move = -1 if sign == "+" else 1
        a2, b2 = (a, b + move) if order == 0 else (a + move, b)
        take((d, h, a, b, q), block(*orient(h, a2, b2), h, q))

    loads[0].wait()
    for h in (0, 1):
        for sign in "+-":
            token_put(h, 0, sign, 0, 0)
    for h in (0, 1):
        for sign in "+-":
            token_put(h, 1, sign, 0, 0)

    def ring_step(name, unit, sign, dist, h):
        way = -1 if sign == "+" else 1
        ref = unit(way * dist, h)
        if dist:
            take((name, sign, dist, h), ref)
        if dist < 3 or (dist == 3 and h == (0 if sign == "+" else 1)):
            dz = step["z" + sign][0]
            put((name, sign, dist + 1, h), ref, ref, at(dz=dz))
        if dist or sign == "+":
            put((name, "c", way * dist, h), ref, ref, at(c=sib))

    def w_unit(dz, h):
        return wq.at[core, pl.ds((z + dz) % NZ * NX + 2 * h, 2)]

    loads[1].wait()
    for dx in (1, 3, 2):
        take(("w", dx), wq.at[core, z * NX + (x - dx) % NX])
    for h in (0, 1):
        for sign in "+-":
            ring_step("W", w_unit, sign, 0, h)

    def w_round(dist, h):
        for sign in "+-":
            ring_step("W", w_unit, sign, dist, h)

    for sign, part in (("+", 0), ("-", 1)):
        for h in (0, 1):
            b = -1 if sign == "+" else 1
            token_take(h, 0, sign, 0, 0)
            token_put(h, 0, sign, 0, b, part)
            for sign2 in "+-":
                token_put(h, 1, sign2, 0, b)
    document_features()
    w_round(1, 0)
    for sign, part in (("+", 0), ("-", 1)):
        for h in (0, 1):
            token_take(h, 1, sign, 0, 0)
            token_put(h, 1, sign, -1 if sign == "+" else 1, 0, part)
    w_round(1, 1)
    for sign, part in (("+", 0), ("-", 1)):
        for h in (0, 1):
            b = -1 if sign == "+" else 1
            token_take(h, 0, sign, 0, b, part)
            for sign2 in "+-":
                token_put(h, 1, sign2, 0, 2 * b, part)
    for sign, part in (("+", 0), ("-", 1)):
        for h in (0, 1):
            token_take(h, 1, sign, -1 if sign == "+" else 1, 0, part)
    w_round(2, 0)
    for b in (-1, 1):
        for sign, part in (("+", 0), ("-", 1)):
            for h in (0, 1):
                token_take(h, 1, sign, 0, b)
                token_put(h, 1, sign, -1 if sign == "+" else 1, b, part)
        w_round(2, 1) if b == -1 else w_round(3, 0)
    for sign, part in (("+", 0), ("-", 1)):
        for h in (0, 1):
            b = -2 if sign == "+" else 2
            token_take(h, 1, sign, 0, b, part)
            token_put(h, 1, sign, -1 if sign == "+" else 1, b, part)
    for sign, part in (("+", 1), ("-", 0)):
        for h in (0, 1):
            token_take(h, 1, sign, 0, -2 if part == 0 else 2, part)
    w_round(3, 1)
    for sign, part in (("+", 0), ("-", 1)):
        a = -1 if sign == "+" else 1
        for b in (-1, 1, 2 * a):
            for h in (0, 1):
                token_take(h, 1, sign, a, b, part)

    def dot(weights, y_list):
        def body(j, carry):
            yy = y_list[0] if len(y_list) == 1 else j // 2
            col = pl.multiple_of(j % 2 * 1024, 1024)
            left = tok[:, pl.ds(yy, 1), :, pl.ds(col, 1024)].reshape(CHUNK, 1024)
            acc[...] += jnp.dot(
                left, weights(yy * 2 + j % 2), preferred_element_type=jnp.float32)
            return carry

        lax.fori_loop(0, 2 * len(y_list), body, 0)

    loads[2].wait()
    loads[3].wait()
    acc[...] = jnp.zeros_like(acc)
    dot(lambda j: wkv[pl.ds(pl.multiple_of(j * 1024, 1024), 1024), :], range(4))
    kv[pl.ds(core * NZ + z, 1)] = acc[...].astype(jnp.bfloat16).reshape(1, CHUNK, 2 * HD)

    def kv_unit(c, dz, h):
        return kv.at[c * NZ + (z + dz) % NZ, pl.ds(h * 256, 256)]

    def kv_copy(ring, dist, sign, h, ref, device):
        return pltpu.make_async_remote_copy(
            src_ref=ref, dst_ref=ref, send_sem=ksend.at[ring, dist, sign, h],
            recv_sem=krecv.at[ring, dist, sign, h], device_id=device, device_id_type=MESH)

    def kv_ring(dist, sign, h, ref):
        return kv_copy(0, dist, sign, h, ref, at(dz=1 if sign == 0 else -1))

    def kv_core(dist, sign, h, ref):
        return kv_copy(1, dist, sign, h, ref, at(c=sib))

    def behind(dist, sign):
        return -dist if sign == 0 else dist

    for h in (0, 1):
        ref = kv_unit(core, 0, h)
        for sign in (0, 1):
            kv_ring(1, sign, h, ref).start()
        kv_core(0, 0, h, ref).start()

    ring_step("W", w_unit, "+", 4, 0)
    ring_step("W", w_unit, "-", 4, 1)
    for dz in (0, -1, 1, -2, 2, -3, 3):
        for h in (0, 1):
            take(("W", "c", dz, h), wq.at[sib, pl.ds((z + dz) % NZ * NX + 2 * h, 2)])
    for dz, h in ((-4, 0), (4, 1)):
        take(("W", "c", dz, h), wq.at[sib, pl.ds((z + dz) % NZ * NX + 2 * h, 2)])

    def q_dot(c):
        acc[...] = jnp.zeros_like(acc)
        dot(lambda j: wq[pl.ds(c, 1), pl.ds(j * 4, 4)].reshape(1024, 256), range(4))
        return (acc[...] * (LOG2E / math.sqrt(HD))).astype(jnp.bfloat16)

    qsend[...] = q_dot(sib)
    put(("Q",), qsend, qland, at(c=sib))
    mine = q_dot(core)
    for g in (0, 1):
        q[pl.ds(core, 1), g, :, :HD] = mine[:, g * HD:(g + 1) * HD].reshape(1, CHUNK, HD)
    take(("Q",), qland)
    for g in (0, 1):
        q[pl.ds(sib, 1), g, :, :HD] = qland[:, g * HD:(g + 1) * HD].reshape(1, CHUNK, HD)
    for h in (0, 1):
        kv_core(0, 0, h, kv_unit(sib, 0, h)).wait_recv()

    def scores_of(piece):
        s, g, blocks = piece
        queries = q[s, g]
        found = []
        for b, diagonal in blocks:
            keys = jnp.concatenate(
                [kv[pl.ds(b, 1), :, :HD], feat[pl.ds(b, 1)]], axis=2).reshape(CHUNK, 2 * HD)
            one = lax.dot_general(
                queries, keys, (((1,), (1,)), ((), ())), preferred_element_type=jnp.float32)
            if diagonal:
                row = lax.broadcasted_iota(jnp.int32, (CHUNK, CHUNK), 0)
                key = lax.broadcasted_iota(jnp.int32, (CHUNK, CHUNK), 1)
                one = jnp.where(key <= row, one, NEG)
            found.append(one)
        return found

    def attend(pieces, fresh=False):
        ahead = scores_of(pieces[0])
        for i, (s, g, blocks) in enumerate(pieces):
            found = ahead
            if i + 1 < len(pieces):
                ahead = scores_of(pieces[i + 1])
            high = jnp.max(functools.reduce(jnp.maximum, found), axis=1, keepdims=True)
            high = jnp.broadcast_to(high, (CHUNK, HD))
            if not fresh:
                old = top[s, g]
                high = jnp.maximum(old, high)
                shrink = jnp.exp2(old - high)
            top[s, g] = high
            wide = jnp.concatenate([high] * (CHUNK // HD), axis=1)
            added = None
            for one, (b, _) in zip(found, blocks):
                weight = jnp.exp2(one - wide).astype(jnp.bfloat16)
                values = jnp.concatenate(
                    [kv[pl.ds(b, 1), :, HD:].reshape(CHUNK, HD),
                     jnp.ones((CHUNK, HD), jnp.bfloat16)], axis=1)
                part = jnp.dot(weight, values, preferred_element_type=jnp.float32)
                added = part if added is None else added + part
            if fresh:
                ctx_acc[s, g] = added
            else:
                ctx_acc[s, g] = (
                    ctx_acc[s, g] * jnp.concatenate([shrink, shrink], axis=1) + added)

    attend([(1, 0, [(z, False), (NZ + z, True)]), (1, 1, [(z, False), (NZ + z, True)]),
            (0, 0, [(z, True)]), (0, 1, [(z, True)])], fresh=True)

    def visit(other):
        earlier = other < z

        @pl.when(earlier)
        def _():
            pair = [(other, False), (NZ + other, False)]
            attend([(1, 0, pair), (1, 1, pair), (0, 0, pair[:1]), (0, 1, pair[:1])])

        @pl.when(jnp.logical_not(earlier))
        def _():
            attend([(1, 0, [(other, False)]), (1, 1, [(other, False)])])

    def kv_round(dist, carry):
        for h in (0, 1):
            for sign in (0, 1):
                ref = kv_unit(core, behind(dist, sign), h)
                kv_ring(dist, sign, h, ref).wait_recv()
                if h == sign:
                    kv_ring(dist + 1, sign, h, ref).start()
                else:
                    @pl.when(dist < 3)
                    def _():
                        kv_ring(dist + 1, sign, h, ref).start()
                kv_core(dist, sign, h, ref).start()
        for h in (0, 1):
            for sign in (0, 1):
                kv_core(dist, sign, h, kv_unit(sib, behind(dist, sign), h)).wait_recv()

        def one(sign, carry):
            visit((z + jnp.where(sign == 0, NZ - dist, dist)) % NZ)
            return carry

        lax.fori_loop(0, 2, one, 0)
        return carry

    lax.fori_loop(1, 4, kv_round, 0)

    for h in (0, 1):
        ref = kv_unit(core, 4, h)
        kv_ring(4, h, h, ref).wait_recv()
        kv_core(4, h, h, ref).start()
    for h in (0, 1):
        kv_core(4, h, h, kv_unit(sib, 4, h)).wait_recv()
    far = (z + 4) % NZ

    def finish(s):
        for g in (0, 1):
            ctx[s, :, g * HD:(g + 1) * HD] = (
                ctx_acc[s, g, :, :HD] / ctx_acc[s, g, :, HD:]).astype(jnp.bfloat16)
        cols = pl.ds(pl.multiple_of(x * 512 + core * 256, 256), 256)
        for dx in (2, 1, 3, 0):
            rows = pl.ds(pl.multiple_of((x + dx) % NX * ROWS, ROWS), ROWS)
            src, dst = ctx.at[s, rows], out_ref.at[:, cols]
            if dx:
                put_out(s, dx, src, dst)
            else:
                @pl.when(core == s)
                def _():
                    pltpu.make_async_copy(src, dst, loc.at[0]).start()

                @pl.when(core != s)
                def _():
                    put_out(s, 0, src, dst)

    def out_copy(s, dx, src, dst):
        i = 4 * core + dx
        return pltpu.make_async_remote_copy(
            src_ref=src, dst_ref=dst, send_sem=osend.at[s, dx], recv_sem=orecv.at[i],
            device_id=at(dx=dx, c=s), device_id_type=MESH)

    def put_out(s, dx, src, dst):
        out_copy(s, dx, src, dst).start()

    @pl.when(far < z)
    def _():
        attend([(0, 0, [(far, False)]), (0, 1, [(far, False)])])

    finish(0)

    @pl.when(far < z)
    def _():
        pair = [(far, False), (NZ + far, False)]
        attend([(1, 0, pair), (1, 1, pair)])

    @pl.when(far >= z)
    def _():
        attend([(1, 0, [(far, False)]), (1, 1, [(far, False)])])

    finish(1)

    def out_land(c, dx):
        return out_ref.at[:, pl.ds(pl.multiple_of((x - dx) % NX * 512 + c * 256, 256), 256)]

    def out_wait(c, dx):
        land = out_land(c, dx)
        pltpu.make_async_remote_copy(
            src_ref=land, dst_ref=land, send_sem=osend.at[0, dx], recv_sem=orecv.at[4 * c + dx],
            device_id=at(c=sib), device_id_type=MESH).wait_recv()

    for c in (0, 1):
        for dx in (1, 2, 3):
            out_wait(c, dx)
    out_wait(sib, 0)
    own = out_land(core, 0)
    pltpu.make_async_copy(own, own, loc.at[0]).wait()

    for copy in sent:
        copy.wait_send()
    piece = ctx.at[0, pl.ds(0, ROWS)]
    for s in (0, 1):
        for dx in (1, 2, 3):
            out_copy(s, dx, piece, piece).wait_send()

        @pl.when(core != s)
        def _():
            out_copy(s, 0, piece, piece).wait_send()
    for h in (0, 1):
        ref = kv_unit(core, 0, h)
        kv_core(0, 0, h, ref).wait_send()
        for sign in (0, 1):
            for dist in (1, 2, 3):
                kv_ring(dist, sign, h, ref).wait_send()
                kv_core(dist, sign, h, ref).wait_send()
        kv_ring(4, h, h, ref).wait_send()
        kv_core(4, h, h, ref).wait_send()


COPIES = 96


def local(tokens, positions, w_query, w_key, w_value):
    anywhere = pl.BlockSpec(memory_space=pltpu.HBM)
    vmem = pl.BlockSpec(memory_space=pltpu.VMEM)
    return pl.pallas_call(
        kernel_body,
        name="layer",
        out_shape=jax.ShapeDtypeStruct((ROWS, 2048), jnp.bfloat16),
        in_specs=[anywhere, vmem, anywhere, anywhere, anywhere],
        out_specs=vmem,
        scratch_shapes=[
            pltpu.VMEM((NX, NY, ROWS, 2048), jnp.bfloat16),
            pltpu.VMEM((2, NZ * NX, 256, 256), jnp.bfloat16),
            pltpu.VMEM((8192, 2 * HD), jnp.bfloat16),
            pltpu.VMEM((2 * NZ, CHUNK, 2 * HD), jnp.bfloat16),
            pltpu.VMEM((2 * NZ, CHUNK, HD), jnp.bfloat16),
            pltpu.VMEM((2, 2, CHUNK, 2 * HD), jnp.bfloat16),
            pltpu.VMEM((CHUNK, 256), jnp.bfloat16),
            pltpu.VMEM((CHUNK, 256), jnp.bfloat16),
            pltpu.VMEM((CHUNK, 256), jnp.float32),
            pltpu.VMEM((64, HD), jnp.float32),
            pltpu.VMEM((2, 2, CHUNK, HD), jnp.float32),
            pltpu.VMEM((2, 2, CHUNK, 2 * HD), jnp.float32),
            pltpu.VMEM((2, CHUNK, 256), jnp.bfloat16),
            pltpu.SemaphoreType.DMA((4,)),
            pltpu.SemaphoreType.DMA((COPIES,)),
            pltpu.SemaphoreType.DMA((COPIES,)),
            pltpu.SemaphoreType.DMA((2, 5, 2, 2)),
            pltpu.SemaphoreType.DMA((2, 5, 2, 2)),
            pltpu.SemaphoreType.DMA((2, 4)),
            pltpu.SemaphoreType.DMA((8,)),
        ],
        compiler_params=pltpu.CompilerParams(
            collective_id=0, has_side_effects=True, vmem_limit_bytes=60 * 2**20),
    )(tokens, positions.reshape(64, HD), w_query, w_key, w_value)


def solution(mesh):
    in_specs = (P(("seq", "row"), "col"), P(), P("row", "col"), P(None, "col"), P(None, "col"))
    out_specs = P(("seq", "row"), "col")
    return jax.shard_map(local, mesh=mesh, in_specs=in_specs, out_specs=out_specs, check_vma=False)
```

```python
import functools
import math

import jax
import jax.numpy as jnp
from jax import lax
from jax.experimental import pallas as pl
from jax.experimental.pallas import tpu as pltpu
from jax.sharding import PartitionSpec as P

HD = 128
NX, NY, NZ = 4, 4, 8
ROWS = 128
CHUNK = NX * ROWS
MESH = pl.DeviceIdType.MESH
LOG2E = 1.4426950408889634
NEG = -1e30
ORDER = (0, 1, 3, 2)


def place():
    row = lax.axis_index("row")
    return lax.axis_index("seq"), row // NX, row % NX, lax.axis_index("col")


def greet(partners):
    barrier = pltpu.get_barrier_semaphore()
    for partner in partners:
        pl.semaphore_signal(barrier, inc=1, device_id=partner, device_id_type=MESH)
    pl.semaphore_wait(barrier, len(partners))


def kernel_body(
    tok_ref, pos_ref, wq_ref, wk_ref, wv_ref, out_ref, tok, wq, wkv, kv, feat, q, qsend, qland, acc,
    docs, top, ctx_acc, ctx, loc, ssem, rsem, ksend, krecv,
    osend, orecv
):
    core, z, x, y = place()
    sib = 1 - core

    def at(dz=0, dx=0, dy=0, c=core):
        return (c, (z + dz) % NZ * NX + (x + dx) % NX, (y + dy) % NY)

    step = {"x+": (0, 1, 0), "x-": (0, -1, 0), "y+": (0, 0, 1), "y-": (0, 0, -1),
            "z+": (1, 0, 0), "z-": (-1, 0, 0)}
    slots = {}
    sent = []

    def slot(key):
        return slots.setdefault(key, len(slots))

    def put(key, src, dst, device):
        i = slot(key)
        copy = pltpu.make_async_remote_copy(
            src_ref=src, dst_ref=dst, send_sem=ssem.at[i], recv_sem=rsem.at[i],
            device_id=device, device_id_type=MESH)
        copy.start()
        sent.append(copy)

    def take(key, dst):
        i = slot(key)
        pltpu.make_async_remote_copy(
            src_ref=dst, dst_ref=dst, send_sem=ssem.at[i], recv_sem=rsem.at[i],
            device_id=at(c=sib), device_id_type=MESH).wait_recv()

    def document_features():
        first = (pos_ref[...] == 0).astype(jnp.bfloat16)
        r = lax.broadcasted_iota(jnp.int32, (HD, HD), 0)
        c = lax.broadcasted_iota(jnp.int32, (HD, HD), 1)
        within = jnp.dot(first, (r <= c).astype(jnp.bfloat16), preferred_element_type=jnp.float32)
        total = jnp.broadcast_to(within[:, HD - 1:], within.shape).astype(jnp.bfloat16)
        before = (c < r).astype(jnp.bfloat16)[:64, :64]
        docs[...] = within + jnp.dot(before, total, preferred_element_type=jnp.float32)

        def body(b, carry):
            for part in range(CHUNK // HD):
                row = docs[pl.ds(b * NX + (x + ORDER[part]) % NX, 1), :]
                hot = jnp.broadcast_to(row, (HD, HD)) == r.astype(jnp.float32)
                feat[pl.ds(b, 1), part * HD:(part + 1) * HD, :] = (
                    hot.astype(jnp.float32).T.astype(jnp.bfloat16).reshape(1, HD, HD))
            return carry

        lax.fori_loop(0, 2 * NZ, body, 0)
        for s in range(2):
            hot = feat[pl.ds(s * NZ + z, 1)].reshape(CHUNK, HD).astype(jnp.float32)
            bar = ((1.0 - hot) * NEG).astype(jnp.bfloat16)
            for g in range(2):
                q[s, g, :, HD:] = bar

    head = x // 2
    my_w = pl.ds(pl.multiple_of(x * 512 + core * 256, 256), 256)
    head_cols = pl.ds(pl.multiple_of(head * HD, HD), HD)
    loads = [
        pltpu.make_async_copy(tok_ref, tok.at[x, y], loc.at[0]),
        pltpu.make_async_copy(wq_ref.at[:, my_w], wq.at[core, z * NX + x], loc.at[1]),
        pltpu.make_async_copy(wk_ref.at[:, head_cols], wkv.at[:, pl.ds(0, HD)], loc.at[2]),
        pltpu.make_async_copy(wv_ref.at[:, head_cols], wkv.at[:, pl.ds(HD, HD)], loc.at[3]),
    ]
    for load in loads:
        load.start()

    greet([at(dx=1), at(dx=2), at(dx=3), at(dy=1), at(dy=3), at(dz=1), at(dz=7), at(c=sib),
           at(dx=1, c=sib), at(dx=2, c=sib), at(dx=3, c=sib)])

    for dx in (1, 3, 2):
        cols = pl.ds(pl.multiple_of((x + dx) % NX * 512 + core * 256, 256), 256)
        put(("w", dx), wq_ref.at[:, cols], wq.at[core, z * NX + x], at(dx=dx))

    def block(u, v, h, q):
        start, size = (h * 64, 64) if q is None else (h * 64 + q * 32, 32)
        return tok.at[(x + u) % NX, (y + v) % NY, pl.ds(start, size)]

    def orient(h, a, b):
        return (a, b) if h == 0 else (b, a)

    def axis(h, order):
        return ("y", "x")[h] if order == 0 else ("x", "y")[h]

    def token_put(h, order, sign, a, b, q=None):
        d = axis(h, order) + sign
        ref = block(*orient(h, a, b), h, q)
        dz, dx, dy = step[d]
        put((d, h, a, b, q), ref, ref, at(dx=dx, dy=dy))

    def token_take(h, order, sign, a, b, q=None):
        d = axis(h, order) + sign
        move = -1 if sign == "+" else 1
        a2, b2 = (a, b + move) if order == 0 else (a + move, b)
        take((d, h, a, b, q), block(*orient(h, a2, b2), h, q))

    loads[0].wait()
    for h in (1, 0):
        for sign in "+-":
            token_put(h, 0, sign, 0, 0)
    for h in (0, 1):
        for sign in "+-":
            token_put(h, 1, sign, 0, 0)

    def dot(dxs, rows, weights):
        acc[rows, :] = jnp.zeros((len(dxs) * ROWS, 256), jnp.float32)

        def body(j, carry):
            col = pl.multiple_of(j % 2 * 1024, 1024)
            left = jnp.concatenate(
                [tok[pl.ds((x + dx) % NX, 1), pl.ds(j // 2, 1), :, pl.ds(col, 1024)].reshape(
                    ROWS, 1024) for dx in dxs], axis=0)
            acc[rows, :] += jnp.dot(left, weights(j), preferred_element_type=jnp.float32)
            return carry

        lax.fori_loop(0, 8, body, 0)
        return acc[rows, :]

    def group_rows(g):
        return pl.ds((0, 128, 384)[g], (128, 256, 128)[g])

    def kv_unit(c, dz, g):
        return kv.at[c * NZ + (z + dz) % NZ, group_rows(g)]

    def behind(dist, sign):
        return -dist if sign == 0 else dist

    def kv_copy(i, dist, sign, ref, device):
        return pltpu.make_async_remote_copy(
            src_ref=ref, dst_ref=ref, send_sem=ksend.at[i, dist, sign],
            recv_sem=krecv.at[i, dist, sign], device_id=device, device_id_type=MESH)

    def kv_ring(g, dist, sign, ref):
        return kv_copy(0, dist, sign, ref, at(dz=1 if sign == 0 else -1))

    def kv_core(g, dist, sign, ref):
        return kv_copy(1, dist, sign, ref, at(c=sib))

    def kv_half(dz, sign):
        return kv.at[core * NZ + (z + dz) % NZ, pl.ds(128 + 128 * sign, 128)]

    def kv_project(g):
        rows = group_rows(g)
        dxs = ((0,), (1, 3), (2,))[g]
        found = dot(dxs, rows, lambda j: wkv[pl.ds(pl.multiple_of(j * 1024, 1024), 1024), :])
        kv[pl.ds(core * NZ + z, 1), rows] = found.astype(jnp.bfloat16).reshape(
            1, len(dxs) * ROWS, 2 * HD)
        ref = kv_unit(core, 0, g)
        for sign in (0, 1):
            if g == 2:
                kv_ring(2, 1, sign, ref).start()
            else:
                put(("K", g, 1, sign), ref, ref, at(dz=1 - 2 * sign))
        if g == 2:
            kv_core(2, 0, 0, ref).start()
        else:
            put(("K", g, "c", 0), ref, ref, at(c=sib))

    def kv_event(g, dist):
        for sign in (0, 1):
            dz = behind(dist, sign)
            if dist == 4:
                if g == 0 and sign == 1:
                    continue
                ref = kv_unit(core, 4, 0) if g == 0 else kv_half(4, sign)
                take(("K", g, 4, sign), ref)
                put(("K", g, "c", 4, sign), ref, ref, at(c=sib))
                continue
            ref = kv_unit(core, dz, g)
            take(("K", g, dist, sign), ref)
            onward = ref
            if dist == 3 and g == 1:
                onward = kv_half(dz, sign)
            if dist < 3 or g == 1 or sign == 0:
                put(("K", g, dist + 1, sign), onward, onward, at(dz=1 - 2 * sign))
            put(("K", g, "c", dz), ref, ref, at(c=sib))

    def kv_core_wait(g, dz):
        if dz == 4:
            for sign in ((0,) if g == 0 else (0, 1)):
                rows = group_rows(0) if g == 0 else pl.ds(128 + 128 * sign, 128)
                take(("K", g, "c", 4, sign), kv.at[sib * NZ + (z + 4) % NZ, rows])
        else:
            take(("K", g, "c", dz), kv_unit(sib, dz, g))

    def q_project(groups, c):
        first = (0, 128, 384)[groups[0]]
        dxs = sum((((0,), (1, 3), (2,))[g] for g in groups), ())
        size = len(dxs) * ROWS
        rows = pl.ds(first, size)
        found = dot(dxs, rows, lambda j: wq[pl.ds(c, 1), pl.ds(j * 4, 4)].reshape(1024, 256))
        found = (found * (LOG2E / math.sqrt(HD))).astype(jnp.bfloat16)
        if c is sib:
            qsend[rows, :] = found
            part = 0 if first == 0 else 1
            put(("Q", part), qsend.at[rows], qland.at[rows], at(c=sib))
        else:
            for g in (0, 1):
                q[pl.ds(core, 1), g, rows, :HD] = found[:, g * HD:(g + 1) * HD].reshape(
                    1, size, HD)

    def ring_step(name, unit, sign, dist, r, plus):
        way = -1 if sign == "+" else 1
        ref = unit(way * dist, r)
        if dist:
            take((name, sign, dist, r), ref)
        if dist < 3 or (dist == 3 and plus == (sign == "+")):
            put((name, sign, dist + 1, r), ref, ref, at(dz=step["z" + sign][0]))
        if dist or sign == "+":
            put((name, "c", way * dist, r), ref, ref, at(c=sib))

    loads[1].wait()

    def w_unit(dz, r):
        return wq.at[core, (z + dz) % NZ * NX + (x + ORDER[r]) % NX]

    def w_event(dist, r):
        for sign in "+-":
            if dist < 4 or sign == ("+" if r < 2 else "-"):
                ring_step("W", w_unit, sign, dist, r, r < 2)

    w_event(0, 0)
    for r, dx in ((1, 3), (2, 1), (3, 2)):
        take(("w", dx), w_unit(0, r))
        w_event(0, r)
    w_event(1, 0)
    for sign, part in (("+", 0), ("-", 1)):
        for h in (0, 1):
            b = -1 if sign == "+" else 1
            token_take(h, 0, sign, 0, 0)
            token_put(h, 0, sign, 0, b, part)
            for sign2 in "+-":
                token_put(h, 1, sign2, 0, b)
    w_event(1, 1)
    document_features()
    w_event(1, 2)
    w_event(1, 3)
    for h in (1, 0):
        for sign, part in (("+", 0), ("-", 1)):
            token_take(h, 1, sign, 0, 0)
            token_put(h, 1, sign, -1 if sign == "+" else 1, 0, part)
    w_event(2, 0)
    for h in (0, 1):
        for sign, part in (("+", 0), ("-", 1)):
            b = -1 if sign == "+" else 1
            token_take(h, 0, sign, 0, b, part)
            if h == 0:
                for sign2 in "+-":
                    token_put(h, 1, sign2, 0, 2 * b, part)
    w_event(2, 1)
    for sign, part in (("+", 0), ("-", 1)):
        token_take(1, 1, sign, -1 if sign == "+" else 1, 0, part)
    loads[2].wait()
    loads[3].wait()
    kv_project(0)
    w_event(2, 2)
    w_event(2, 3)
    for h in (1, 0):
        for b in (-1, 1):
            for sign, part in (("+", 0), ("-", 1)):
                token_take(h, 1, sign, 0, b)
                token_put(h, 1, sign, -1 if sign == "+" else 1, b, part)
        if h == 1:
            for sign, part in (("+", 0), ("-", 1)):
                for sign2 in "+-":
                    token_put(h, 1, sign2, 0, -2 if sign == "+" else 2, part)
        w_event(3, 1 - h)
    kv_event(0, 1)
    w_event(3, 2)
    for sign, part in (("+", 0), ("-", 1)):
        b = -2 if sign == "+" else 2
        token_take(0, 1, sign, 0, b, part)
        token_put(0, 1, sign, -1 if sign == "+" else 1, b, part)
    for sign, part in (("+", 1), ("-", 0)):
        token_take(0, 1, sign, 0, -2 if part == 0 else 2, part)
    w_event(3, 3)
    kv_event(0, 2)
    for sign, part in (("+", 0), ("-", 1)):
        for b in (-1, 1):
            token_take(1, 1, sign, -1 if sign == "+" else 1, b, part)
    kv_project(1)
    for sign, part in (("+", 0), ("-", 1)):
        b = -2 if sign == "+" else 2
        token_take(1, 1, sign, 0, b, part)
        token_put(1, 1, sign, -1 if sign == "+" else 1, b, part)
    kv_event(0, 3)
    for r in range(4):
        w_event(4, r)
    kv_event(1, 1)
    kv_event(0, 4)
    for dz in (0, -1, 1, -2, 2, -3, 3, 4):
        for r in range(4):
            key = dz if abs(dz) < 4 else (-4 if r < 2 else 4)
            take(("W", "c", key, r), wq.at[sib, (z + dz) % NZ * NX + (x + ORDER[r]) % NX])
    q_project((0, 1), sib)
    kv_event(1, 2)
    q_project((0, 1), core)
    kv_event(1, 3)
    for sign, part in (("+", 1), ("-", 0)):
        token_take(1, 1, sign, 0, -2 if part == 0 else 2, part)
    for sign, part in (("+", 0), ("-", 1)):
        a = -1 if sign == "+" else 1
        for b in (0, -1, 1, 2 * a):
            token_take(0, 1, sign, a, b, part)
        token_take(1, 1, sign, a, 2 * a, part)
    kv_project(2)
    q_project((2,), sib)
    q_project((2,), core)
    kv_event(1, 4)
    for r in (0, 1):
        rows = pl.ds((0, 384)[r], (384, 128)[r])
        take(("Q", r), qland.at[rows])
    for g in (0, 1):
        q[pl.ds(sib, 1), g, :, :HD] = qland[:, g * HD:(g + 1) * HD].reshape(1, CHUNK, HD)
    for g in (0, 1):
        for dz in (0, -1, 1, -2, 2, -3, 3, 4):
            kv_core_wait(g, dz)
    kv_core(2, 0, 0, kv_unit(sib, 0, 2)).wait_recv()

    def places(dim):
        size = (HD, CHUNK) if dim == 0 else (CHUNK, HD)
        return jnp.concatenate(
            [lax.broadcasted_iota(jnp.int32, size, dim) + (x + dx) % NX * ROWS for dx in ORDER],
            axis=dim)

    def scores_of(piece):
        s, g, blocks = piece
        queries = q[s, g]
        found = []
        for b, diagonal in blocks:
            keys = jnp.concatenate(
                [kv[pl.ds(b, 1), :, :HD], feat[pl.ds(b, 1)]], axis=2).reshape(CHUNK, 2 * HD)
            one = lax.dot_general(
                queries, keys, (((1,), (1,)), ((), ())), preferred_element_type=jnp.float32)
            if diagonal:
                one = jnp.where(places(1) <= places(0), one, NEG)
            found.append(one)
        return found

    def attend(pieces, fresh=False):
        ahead = scores_of(pieces[0])
        for i, (s, g, blocks) in enumerate(pieces):
            found = ahead
            if i + 1 < len(pieces):
                ahead = scores_of(pieces[i + 1])
            high = jnp.max(functools.reduce(jnp.maximum, found), axis=1, keepdims=True)
            high = jnp.broadcast_to(high, (CHUNK, HD))
            if not fresh:
                old = top[s, g]
                high = jnp.maximum(old, high)
                shrink = jnp.exp2(old - high)
            top[s, g] = high
            wide = jnp.concatenate([high] * (CHUNK // HD), axis=1)
            added = None
            for one, (b, _) in zip(found, blocks):
                weight = jnp.exp2(one - wide).astype(jnp.bfloat16)
                values = jnp.concatenate(
                    [kv[pl.ds(b, 1), :, HD:].reshape(CHUNK, HD),
                     jnp.ones((CHUNK, HD), jnp.bfloat16)], axis=1)
                part = jnp.dot(weight, values, preferred_element_type=jnp.float32)
                added = part if added is None else added + part
            if fresh:
                ctx_acc[s, g] = added
            else:
                ctx_acc[s, g] = (
                    ctx_acc[s, g] * jnp.concatenate([shrink, shrink], axis=1) + added)

    attend([(1, 0, [(z, False), (NZ + z, True)]), (1, 1, [(z, False), (NZ + z, True)]),
            (0, 0, [(z, True)]), (0, 1, [(z, True)])], fresh=True)

    def kv_round(dist, carry):
        for sign in (0, 1):
            ref = kv_unit(core, behind(dist, sign), 2)
            kv_ring(2, dist, sign, ref).wait_recv()
            if sign == 1:
                kv_ring(2, dist + 1, sign, ref).start()
            else:
                @pl.when(dist < 3)
                def _():
                    kv_ring(2, dist + 1, sign, ref).start()
            kv_core(2, dist, sign, ref).start()
        for sign in (0, 1):
            kv_core(2, dist, sign, kv_unit(sib, behind(dist, sign), 2)).wait_recv()
        low, high = (z + NZ - dist) % NZ, (z + dist) % NZ
        both = [(low, False), (high, False)]
        first = [(1, 0, both), (1, 1, both)]
        count = jnp.where(low < z, 1, 0) + jnp.where(high < z, 1, 0)

        @pl.when(count == 0)
        def _():
            attend(first)

        @pl.when(count == 1)
        def _():
            one = [(jnp.where(low < z, low, high), False)]
            attend(first + [(0, 0, one), (0, 1, one)])

        @pl.when(count == 2)
        def _():
            attend(first + [(0, 0, both), (0, 1, both)])

        return carry

    lax.fori_loop(1, 4, kv_round, 0)

    ref = kv_unit(core, 4, 2)
    kv_ring(2, 4, 1, ref).wait_recv()
    kv_core(2, 4, 1, ref).start()
    kv_core(2, 4, 1, kv_unit(sib, 4, 2)).wait_recv()
    far = (z + 4) % NZ

    def finish(s):
        for g in (0, 1):
            ctx[s, :, g * HD:(g + 1) * HD] = (
                ctx_acc[s, g, :, :HD] / ctx_acc[s, g, :, HD:]).astype(jnp.bfloat16)
        cols = pl.ds(pl.multiple_of(x * 512 + core * 256, 256), 256)
        for r in (3, 1, 2, 0):
            src, dst = ctx.at[s, pl.ds(r * ROWS, ROWS)], out_ref.at[:, cols]
            if r:
                out_copy(s, ORDER[r], src, dst).start()
            else:
                @pl.when(core == s)
                def _():
                    pltpu.make_async_copy(src, dst, loc.at[0]).start()

                @pl.when(core != s)
                def _():
                    out_copy(s, 0, src, dst).start()

    def out_copy(s, dx, src, dst):
        return pltpu.make_async_remote_copy(
            src_ref=src, dst_ref=dst, send_sem=osend.at[s, dx], recv_sem=orecv.at[4 * core + dx],
            device_id=at(dx=dx, c=s), device_id_type=MESH)

    @pl.when(far < z)
    def _():
        one = [(far, False)]
        attend([(0, 0, one), (0, 1, one), (1, 0, one), (1, 1, one)])

    @pl.when(far >= z)
    def _():
        attend([(1, 0, [(far, False)]), (1, 1, [(far, False)])])

    finish(0)

    def pair(i, carry):
        two = [(NZ + 2 * i, False), (NZ + 2 * i + 1, False)]
        attend([(1, 0, two), (1, 1, two)])
        return carry

    lax.fori_loop(0, z // 2, pair, 0)

    @pl.when(z % 2 == 1)
    def _():
        one = [(NZ + z - 1, False)]
        attend([(1, 0, one), (1, 1, one)])

    finish(1)

    def out_land(c, dx):
        return out_ref.at[:, pl.ds(pl.multiple_of((x - dx) % NX * 512 + c * 256, 256), 256)]

    def out_wait(c, dx):
        land = out_land(c, dx)
        pltpu.make_async_remote_copy(
            src_ref=land, dst_ref=land, send_sem=osend.at[0, dx], recv_sem=orecv.at[4 * c + dx],
            device_id=at(c=sib), device_id_type=MESH).wait_recv()

    for c in (0, 1):
        for dx in (1, 2, 3):
            out_wait(c, dx)
    out_wait(sib, 0)
    own = out_land(core, 0)
    pltpu.make_async_copy(own, own, loc.at[0]).wait()

    for copy in sent:
        copy.wait_send()
    piece = ctx.at[0, pl.ds(0, ROWS)]
    for s in (0, 1):
        for dx in (1, 2, 3):
            out_copy(s, dx, piece, piece).wait_send()

        @pl.when(core != s)
        def _():
            out_copy(s, 0, piece, piece).wait_send()
    ref = kv_unit(core, 0, 2)
    kv_core(2, 0, 0, ref).wait_send()
    for sign in (0, 1):
        for dist in (1, 2, 3):
            kv_ring(2, dist, sign, ref).wait_send()
            kv_core(2, dist, sign, ref).wait_send()
    kv_ring(2, 4, 1, ref).wait_send()
    kv_core(2, 4, 1, ref).wait_send()


COPIES = 168


def local(tokens, positions, w_query, w_key, w_value):
    anywhere = pl.BlockSpec(memory_space=pltpu.HBM)
    vmem = pl.BlockSpec(memory_space=pltpu.VMEM)
    return pl.pallas_call(
        kernel_body,
        name="layer",
        out_shape=jax.ShapeDtypeStruct((ROWS, 2048), jnp.bfloat16),
        in_specs=[anywhere, vmem, anywhere, anywhere, anywhere],
        out_specs=vmem,
        scratch_shapes=[
            pltpu.VMEM((NX, NY, ROWS, 2048), jnp.bfloat16),
            pltpu.VMEM((2, NZ * NX, 256, 256), jnp.bfloat16),
            pltpu.VMEM((8192, 2 * HD), jnp.bfloat16),
            pltpu.VMEM((2 * NZ, CHUNK, 2 * HD), jnp.bfloat16),
            pltpu.VMEM((2 * NZ, CHUNK, HD), jnp.bfloat16),
            pltpu.VMEM((2, 2, CHUNK, 2 * HD), jnp.bfloat16),
            pltpu.VMEM((CHUNK, 256), jnp.bfloat16),
            pltpu.VMEM((CHUNK, 256), jnp.bfloat16),
            pltpu.VMEM((CHUNK, 256), jnp.float32),
            pltpu.VMEM((64, HD), jnp.float32),
            pltpu.VMEM((2, 2, CHUNK, HD), jnp.float32),
            pltpu.VMEM((2, 2, CHUNK, 2 * HD), jnp.float32),
            pltpu.VMEM((2, CHUNK, 256), jnp.bfloat16),
            pltpu.SemaphoreType.DMA((4,)),
            pltpu.SemaphoreType.DMA((COPIES,)),
            pltpu.SemaphoreType.DMA((COPIES,)),
            pltpu.SemaphoreType.DMA((2, 5, 2)),
            pltpu.SemaphoreType.DMA((2, 5, 2)),
            pltpu.SemaphoreType.DMA((2, 4)),
            pltpu.SemaphoreType.DMA((8,)),
        ],
        compiler_params=pltpu.CompilerParams(
            collective_id=0, has_side_effects=True, vmem_limit_bytes=60 * 2**20),
    )(tokens, positions.reshape(64, HD), w_query, w_key, w_value)


def solution(mesh):
    in_specs = (P(("seq", "row"), "col"), P(), P("row", "col"), P(None, "col"), P(None, "col"))
    out_specs = P(("seq", "row"), "col")
    return jax.shard_map(local, mesh=mesh, in_specs=in_specs, out_specs=out_specs, check_vma=False)
```

```python
import functools
import math

import jax
import jax.numpy as jnp
from jax import lax
from jax.experimental import pallas as pl
from jax.experimental.pallas import tpu as pltpu
from jax.sharding import PartitionSpec as P

HD = 128
NX, NY, NZ = 4, 4, 8
ROWS = 128
CHUNK = NX * ROWS
MESH = pl.DeviceIdType.MESH
LOG2E = 1.4426950408889634
NEG = -1e30
ORDER = (0, 1, 3, 2)


def place():
    row = lax.axis_index("row")
    return lax.axis_index("seq"), row // NX, row % NX, lax.axis_index("col")


def greet(partners):
    barrier = pltpu.get_barrier_semaphore()
    for partner in partners:
        pl.semaphore_signal(barrier, inc=1, device_id=partner, device_id_type=MESH)
    pl.semaphore_wait(barrier, len(partners))

DEFER = (True, True)

PLAN = (
    "feat", ("w", 1), ("w", 3), ("W", 1, 1, 0), ("W", -1, 1, 0), ("t", 0, 0, 1, 0, 0, -1),
    ("t", 0, 0, -1, 0, 0, -1), ("w", 2), ("W", 1, 1, 2), ("W", -1, 1, 2), ("W", 1, 1, 1),
    ("W", -1, 1, 1), ("t", 1, 0, 1, 0, 0, -1), ("t", 1, 0, -1, 0, 0, -1),
    ("t", 1, 1, 1, 0, 0, -1), ("t", 1, 1, -1, 0, 0, -1), ("W", 1, 2, 0), ("W", -1, 2, 0),
    ("t", 0, 0, 1, 0, -1, 0), ("t", 0, 0, -1, 0, 1, 1), ("W", 1, 1, 3), ("W", -1, 1, 3),
    ("t", 0, 1, 1, 0, 0, -1), ("t", 0, 1, -1, 0, 0, -1), ("W", 1, 2, 2), ("W", -1, 2, 2), "kv",
    ("W", 1, 2, 1), ("W", -1, 2, 1), ("t", 0, 1, 1, 0, -1, -1), ("t", 0, 1, -1, 0, -1, -1),
    ("t", 1, 1, 1, 0, -1, -1), ("t", 1, 1, -1, 0, -1, -1), ("W", 1, 3, 0), ("W", -1, 3, 0),
    ("W", 1, 2, 3), ("W", -1, 2, 3), ("t", 0, 1, 1, 0, 1, -1), ("t", 0, 1, -1, 0, 1, -1),
    ("t", 1, 1, 1, 0, 1, -1), ("t", 1, 1, -1, 0, 1, -1), ("W", 1, 3, 2), ("W", -1, 3, 2),
    ("t", 1, 0, 1, 0, -1, 0), ("t", 1, 0, -1, 0, 1, 1), ("K", 1, 1, 0), ("K", -1, 1, 0),
    ("t", 0, 1, 1, 0, -2, 0), ("W", 1, 3, 1), ("W", -1, 3, 1), ("t", 0, 1, -1, 0, 2, 1),
    ("t", 1, 1, 1, 0, -2, 0), ("W", 1, 4, 0), ("W", -1, 3, 3), ("t", 1, 1, -1, 0, 2, 1),
    ("W", 1, 3, 3), ("W", -1, 4, 2), ("kx", 1), ("kx", 3), ("K", 1, 2, 0), ("K", -1, 2, 0),
    ("kx", 2), ("W", 1, 4, 1), ("W", -1, 4, 3), ("K", 1, 1, 2), ("K", -1, 1, 2), ("K", 1, 1, 1),
    ("K", -1, 1, 1), "q01s", ("K", 1, 3, 0), ("K", -1, 3, 0), "q01c", ("K", 1, 1, 3),
    ("K", -1, 1, 3), ("K", 1, 2, 2), ("K", -1, 2, 2), "q2s", ("K", 1, 2, 1), ("K", -1, 2, 1),
    "q2c", ("K", 1, 4, 0),
)
LATE = (
    (("K", -1, 2, 3), ("K", 1, 2, 3), ("K", -1, 3, 2), ("K", 1, 3, 2), ),
    (("K", -1, 3, 1), ("K", 1, 3, 1), ("K", -1, 3, 3), ("K", 1, 3, 3), ),
    (("K", -1, 4, 2), ),
    (("K", 1, 4, 1), ("K", -1, 4, 3), ),
)

FROM = {1: 3, 2: 1, 3: 2}


def token_moves():
    t = "t"
    moves = {}
    beside = [(t, 1, 1, s, 0, 0, -1) for s in (1, -1)]
    next_to = [(t, 1, 1, s, 0, b, -1) for s in (1, -1) for b in (1, -1)]
    for h in (0, 1):
        for s in (1, -1):
            moves[t, h, h, s, 0, 0, -1] = ()
    for h in (1, 0):
        for s in (1, -1):
            moves[t, h, 1 - h, s, 0, 0, -1] = ()
    for h in (0, 1):
        for s, p in ((1, 0), (-1, 1)):
            moves[t, h, 0, s, 0, -s, p] = ((t, h, 0, s, 0, 0, -1),)
        for s, p in ((1, 0), (-1, 1)):
            moves[t, h, 1, s, -s, 0, p] = ((t, h, 1, s, 0, 0, -1),)
        for s, p in ((1, 0), (-1, 1)):
            for s2 in (1, -1):
                moves[t, h, 1, s2, 0, -s, -1] = (
                    (t, h, 0, s, 0, 0, -1),) + tuple(beside if h and DEFER[0] else ())
        for s, p in ((1, 0), (-1, 1)):
            for b in (1, -1):
                moves[t, h, 1, s, -s, b, p] = ((t, h, 1, s, 0, b, -1),)
        for s, p in ((1, 0), (-1, 1)):
            for s2 in (1, -1):
                moves[t, h, 1, s2, 0, -2 * s, p] = (
                    (t, h, 0, s, 0, -s, p),) + tuple(next_to if h and DEFER[1] else ())
        for s, p in ((1, 0), (-1, 1)):
            moves[t, h, 1, s, -s, -2 * s, p] = ((t, h, 1, s, 0, -2 * s, p),)
    return moves


def ring_moves(name, first):
    moves = {}
    for r in range(4):
        for s in (1, -1):
            moves[name, s, 1, r] = first[r]
        moves[name + "c", 0, r] = first[r]
    for dist in (1, 2, 3, 4):
        for r in range(4):
            for s in (1, -1):
                if dist < 3 or (dist == 3 and s == (1 if r < 2 else -1)):
                    moves[name, s, dist + 1, r] = ((name, s, dist, r),)
                if dist < 4 or s == (1 if r < 2 else -1):
                    moves[name + "c", -s * dist, r] = ((name, s, dist, r),)
    return moves


def all_moves():
    moves = {("w", dx): () for dx in (1, 3, 2)}
    moves.update(token_moves())
    moves.update(ring_moves("W", [()] + [(("w", FROM[r]),) for r in (1, 2, 3)]))
    moves.update({("kx", dx): ("kv",) for dx in (1, 3, 2)})
    moves.update(ring_moves("K", [("kv",)] + [(("kx", FROM[r]),) for r in (1, 2, 3)]))
    return moves


def kernel_body(
    tok_ref, pos_ref, wq_ref, wk_ref, wv_ref, out_ref, tok, wq, wkv, kvacc, kvown, kv, feat, q, qsend, qland, acc,
    docs, top, ctx_acc, ctx, loc, ssem, rsem,
    qsem, osend, orecv
):
    core, z, x, y = place()
    sib = 1 - core

    def at(dz=0, dx=0, dy=0, c=core):
        return (c, (z + dz) % NZ * NX + (x + dx) % NX, (y + dy) % NY)

    moves = all_moves()
    slots = {key: i for i, key in enumerate(moves)}
    done, sent = set(), set()

    def block(h, a, b, part):
        u, v = (a, b) if h == 0 else (b, a)
        start, size = (h * 64, 64) if part < 0 else (h * 64 + part * 32, 32)
        return tok.at[(x + u) % NX, (y + v) % NY, pl.ds(start, size)]

    def w_unit(dz, r, c=core):
        return wq.at[c, (z + dz) % NZ * NX + (x + ORDER[r]) % NX]

    def kv_unit(dz, r, c=core):
        return kv.at[c * NZ + (z + dz) % NZ, pl.ds(r * ROWS, ROWS)]

    def ends(key):
        kind = key[0]
        if kind == "t":
            _, h, order, s, a, b, part = key
            src = block(h, a, b, part)
            land = block(h, a, b - s, part) if order == 0 else block(h, a - s, b, part)
            return src, src, at(dy=s) if h == order else at(dx=s), land
        if kind == "w":
            dx = key[1]
            cols = pl.ds(pl.multiple_of((x + dx) % NX * 512 + core * 256, 256), 256)
            return wq_ref.at[:, cols], w_unit(0, 0), at(dx=dx), w_unit(0, ORDER.index(NX - dx))
        if kind == "kx":
            dx = key[1]
            land = kv_unit(0, ORDER.index(NX - dx))
            return kvown.at[(x + dx) % NX // 2], land, at(dx=dx), land
        unit = w_unit if kind[0] == "W" else kv_unit
        if kind[1:] == "c":
            src = unit(key[1], key[2])
            return src, src, at(c=sib), unit(key[1], key[2], sib)
        _, s, dist, r = key
        src = unit(-s * (dist - 1), r)
        return src, src, at(dz=s), unit(-s * dist, r)

    def copy_of(key):
        src, dst, device, _ = ends(key)
        i = slots[key]
        return pltpu.make_async_remote_copy(
            src_ref=src, dst_ref=dst, send_sem=ssem.at[i], recv_sem=rsem.at[i],
            device_id=device, device_id_type=MESH)

    def fire():
        for key, needs in moves.items():
            if key not in sent and all(need in done for need in needs):
                sent.add(key)
                copy_of(key).start()

    def take(key):
        if key in done:
            return
        land = ends(key)[3]
        i = slots[key]
        pltpu.make_async_remote_copy(
            src_ref=land, dst_ref=land, send_sem=ssem.at[i], recv_sem=rsem.at[i],
            device_id=at(c=sib), device_id_type=MESH).wait_recv()
        done.add(key)
        fire()

    def take_tokens(offsets):
        for key in moves:
            if key[0] == "t":
                _, h, order, s, a, b, _ = key
                a, b = (a, b - s) if order == 0 else (a - s, b)
                if (a if h == 0 else b) % NX in offsets:
                    take(key)

    def document_features():
        first = (pos_ref[...] == 0).astype(jnp.bfloat16)
        r = lax.broadcasted_iota(jnp.int32, (HD, HD), 0)
        c = lax.broadcasted_iota(jnp.int32, (HD, HD), 1)
        within = jnp.dot(first, (r <= c).astype(jnp.bfloat16), preferred_element_type=jnp.float32)
        total = jnp.broadcast_to(within[:, HD - 1:], within.shape).astype(jnp.bfloat16)
        before = (c < r).astype(jnp.bfloat16)[:64, :64]
        docs[...] = within + jnp.dot(before, total, preferred_element_type=jnp.float32)

        def body(b, carry):
            for part in range(CHUNK // HD):
                row = docs[pl.ds(b * NX + (x + ORDER[part]) % NX, 1), :]
                hot = jnp.broadcast_to(row, (HD, HD)) == r.astype(jnp.float32)
                feat[pl.ds(b, 1), part * HD:(part + 1) * HD, :] = (
                    hot.astype(jnp.float32).T.astype(jnp.bfloat16).reshape(1, HD, HD))
            return carry

        lax.fori_loop(0, 2 * NZ, body, 0)
        for s in range(2):
            hot = feat[pl.ds(s * NZ + z, 1)].reshape(CHUNK, HD).astype(jnp.float32)
            bar = ((1.0 - hot) * NEG).astype(jnp.bfloat16)
            for g in range(2):
                q[s, g, :, HD:] = bar

    my_w = pl.ds(pl.multiple_of(x * 512 + core * 256, 256), 256)
    loads = [
        pltpu.make_async_copy(tok_ref, tok.at[x, y], loc.at[0]),
        pltpu.make_async_copy(wq_ref.at[:, my_w], wq.at[core, z * NX + x], loc.at[1]),
    ]
    for i in range(4):
        source = (wk_ref, wv_ref)[i % 2].at[:, pl.ds(i // 2 * HD, HD)]
        loads.append(pltpu.make_async_copy(source, wkv.at[:, pl.ds(i * HD, HD)], loc.at[2 + i]))
    for load in loads:
        load.start()

    greet([at(dx=1), at(dx=2), at(dx=3), at(dy=1), at(dy=3), at(dz=1), at(dz=7), at(c=sib),
           at(dx=1, c=sib), at(dx=2, c=sib), at(dx=3, c=sib)])

    loads[0].wait()
    loads[1].wait()
    fire()

    def dot(dxs, rows, weights):
        acc[rows, :] = jnp.zeros((len(dxs) * ROWS, 256), jnp.float32)

        def body(j, carry):
            col = pl.multiple_of(j % 2 * 1024, 1024)
            left = jnp.concatenate(
                [tok[pl.ds((x + dx) % NX, 1), pl.ds(j // 2, 1), :, pl.ds(col, 1024)].reshape(
                    ROWS, 1024) for dx in dxs], axis=0)
            acc[rows, :] += jnp.dot(left, weights(j), preferred_element_type=jnp.float32)
            return carry

        lax.fori_loop(0, 8, body, 0)
        return acc[rows, :]

    def kv_project():
        kvacc[...] = jnp.zeros_like(kvacc)

        def body(j, carry):
            left = tok[pl.ds(x, 1), pl.ds(j // 2, 1), :,
                       pl.ds(pl.multiple_of(j % 2 * 1024, 1024), 1024)].reshape(ROWS, 1024)
            kvacc[...] += jnp.dot(
                left, wkv[pl.ds(pl.multiple_of(j * 1024, 1024), 1024), :],
                preferred_element_type=jnp.float32)
            return carry

        lax.fori_loop(0, 8, body, 0)
        for head in (0, 1):
            kvown[head] = kvacc[:, head * 256:head * 256 + 256].astype(jnp.bfloat16)
        kv[pl.ds(core * NZ + z, 1), 0:ROWS] = kvown[pl.ds(x // 2, 1)]

    def q_copy(i):
        rows = pl.ds((0, 384)[i], (384, 128)[i])
        return pltpu.make_async_remote_copy(
            src_ref=qsend.at[rows], dst_ref=qland.at[rows], send_sem=qsem.at[0, i],
            recv_sem=qsem.at[1, i], device_id=at(c=sib), device_id_type=MESH)

    def q_project(groups, c):
        first = (0, 128, 384)[groups[0]]
        dxs = sum((((0,), (1, 3), (2,))[g] for g in groups), ())
        size = len(dxs) * ROWS
        rows = pl.ds(first, size)
        found = dot(dxs, rows, lambda j: wq[pl.ds(c, 1), pl.ds(j * 4, 4)].reshape(1024, 256))
        found = (found * (LOG2E / math.sqrt(HD))).astype(jnp.bfloat16)
        if c is sib:
            qsend[rows, :] = found
            q_copy(0 if first == 0 else 1).start()
        else:
            for g in (0, 1):
                q[pl.ds(core, 1), g, rows, :HD] = found[:, g * HD:(g + 1) * HD].reshape(
                    1, size, HD)

    def ring_step(name, unit, sign, dist, r, plus):
        way = -1 if sign == "+" else 1
        ref = unit(way * dist, r)
        if dist:
            take((name, sign, dist, r), ref)
        if dist < 3 or (dist == 3 and plus == (sign == "+")):
            put((name, sign, dist + 1, r), ref, ref, at(dz=step["z" + sign][0]))
        if dist or sign == "+":
            put((name, "c", way * dist, r), ref, ref, at(c=sib))

    def kv_core_wait(dist):
        for key in moves:
            if key[0] == "Kc" and abs(key[1]) == dist:
                take(key)

    for entry in PLAN:
        if entry == "feat":
            document_features()
        elif entry == "kv":
            take_tokens((0,))
            for load in loads[2:]:
                load.wait()
            kv_project()
            done.add("kv")
            fire()
        elif entry == "q01s":
            take_tokens((0, 1, 3))
            for key in moves:
                if key[0][0] == "W":
                    take(key)
            q_project((0, 1), sib)
        elif entry == "q01c":
            q_project((0, 1), core)
        elif entry == "q2s":
            take_tokens((2,))
            q_project((2,), sib)
        elif entry == "q2c":
            q_project((2,), core)
        else:
            take(entry)
    for i in (0, 1):
        q_copy(i).wait_recv()
    for g in (0, 1):
        q[pl.ds(sib, 1), g, :, :HD] = qland[:, g * HD:(g + 1) * HD].reshape(1, CHUNK, HD)
    kv_core_wait(0)

    def places(dim):
        size = (HD, CHUNK) if dim == 0 else (CHUNK, HD)
        return jnp.concatenate(
            [lax.broadcasted_iota(jnp.int32, size, dim) + (x + dx) % NX * ROWS for dx in ORDER],
            axis=dim)

    def scores_of(piece):
        s, g, blocks = piece
        queries = q[s, g]
        found = []
        for b, diagonal in blocks:
            keys = jnp.concatenate(
                [kv[pl.ds(b, 1), :, :HD], feat[pl.ds(b, 1)]], axis=2).reshape(CHUNK, 2 * HD)
            one = lax.dot_general(
                queries, keys, (((1,), (1,)), ((), ())), preferred_element_type=jnp.float32)
            if diagonal:
                one = jnp.where(places(1) <= places(0), one, NEG)
            found.append(one)
        return found

    def attend(pieces, fresh=False):
        ahead = scores_of(pieces[0])
        for i, (s, g, blocks) in enumerate(pieces):
            found = ahead
            if i + 1 < len(pieces):
                ahead = scores_of(pieces[i + 1])
            high = jnp.max(functools.reduce(jnp.maximum, found), axis=1, keepdims=True)
            high = jnp.broadcast_to(high, (CHUNK, HD))
            if not fresh:
                old = top[s, g]
                high = jnp.maximum(old, high)
                shrink = jnp.exp2(old - high)
            top[s, g] = high
            wide = jnp.concatenate([high] * (CHUNK // HD), axis=1)
            added = None
            for one, (b, _) in zip(found, blocks):
                weight = jnp.exp2(one - wide).astype(jnp.bfloat16)
                values = jnp.concatenate(
                    [kv[pl.ds(b, 1), :, HD:].reshape(CHUNK, HD),
                     jnp.ones((CHUNK, HD), jnp.bfloat16)], axis=1)
                part = jnp.dot(weight, values, preferred_element_type=jnp.float32)
                added = part if added is None else added + part
            if fresh:
                ctx_acc[s, g] = added
            else:
                ctx_acc[s, g] = (
                    ctx_acc[s, g] * jnp.concatenate([shrink, shrink], axis=1) + added)

    def finish(s):
        for g in (0, 1):
            ctx[s, :, g * HD:(g + 1) * HD] = (
                ctx_acc[s, g, :, :HD] / ctx_acc[s, g, :, HD:]).astype(jnp.bfloat16)
        cols = pl.ds(pl.multiple_of(x * 512 + core * 256, 256), 256)
        for r in (3, 1, 2, 0):
            src, dst = ctx.at[s, pl.ds(r * ROWS, ROWS)], out_ref.at[:, cols]
            if r:
                out_copy(s, ORDER[r], src, dst).start()
            else:
                @pl.when(core == s)
                def _():
                    pltpu.make_async_copy(src, dst, loc.at[0]).start()

                @pl.when(core != s)
                def _():
                    out_copy(s, 0, src, dst).start()

    def out_copy(s, dx, src, dst):
        return pltpu.make_async_remote_copy(
            src_ref=src, dst_ref=dst, send_sem=osend.at[s, dx], recv_sem=orecv.at[4 * core + dx],
            device_id=at(dx=dx, c=s), device_id_type=MESH)

    attend([(1, 0, [(z, False), (NZ + z, True)]), (1, 1, [(z, False), (NZ + z, True)]),
            (0, 0, [(z, True)]), (0, 1, [(z, True)])], fresh=True)

    @pl.when(z == 0)
    def _():
        finish(0)

    def kv_round(dist, carry):
        for now in (1, 2, 3):
            @pl.when(dist == now)
            def _():
                for key in LATE[now - 1]:
                    take(key)
                kv_core_wait(now)

        low, high = (z + NZ - dist) % NZ, (z + dist) % NZ
        both = [(low, False), (high, False)]
        first = [(1, 0, both), (1, 1, both)]
        count = jnp.where(low < z, 1, 0) + jnp.where(high < z, 1, 0)

        @pl.when(count == 0)
        def _():
            attend(first)

        @pl.when(count == 1)
        def _():
            one = [(jnp.where(low < z, low, high), False)]
            attend(first + [(0, 0, one), (0, 1, one)])

        @pl.when(count == 2)
        def _():
            attend(first + [(0, 0, both), (0, 1, both)])

        @pl.when(dist == z)
        def _():
            finish(0)

        return carry

    lax.fori_loop(1, 4, kv_round, 0)

    for key in LATE[3]:
        take(key)
    kv_core_wait(4)
    far = (z + 4) % NZ

    @pl.when(far < z)
    def _():
        one = [(far, False)]
        attend([(0, 0, one), (0, 1, one), (1, 0, one), (1, 1, one)])

    @pl.when(far >= z)
    def _():
        attend([(1, 0, [(far, False)]), (1, 1, [(far, False)])])

    @pl.when(z > 3)
    def _():
        finish(0)

    def pair(i, carry):
        two = [(NZ + 2 * i, False), (NZ + 2 * i + 1, False)]
        attend([(1, 0, two), (1, 1, two)])
        return carry

    lax.fori_loop(0, z // 2, pair, 0)

    @pl.when(z % 2 == 1)
    def _():
        one = [(NZ + z - 1, False)]
        attend([(1, 0, one), (1, 1, one)])

    finish(1)

    def out_land(c, dx):
        return out_ref.at[:, pl.ds(pl.multiple_of((x - dx) % NX * 512 + c * 256, 256), 256)]

    def out_wait(c, dx):
        land = out_land(c, dx)
        pltpu.make_async_remote_copy(
            src_ref=land, dst_ref=land, send_sem=osend.at[0, dx], recv_sem=orecv.at[4 * c + dx],
            device_id=at(c=sib), device_id_type=MESH).wait_recv()

    for c in (0, 1):
        for dx in (1, 2, 3):
            out_wait(c, dx)
    out_wait(sib, 0)
    own = out_land(core, 0)
    pltpu.make_async_copy(own, own, loc.at[0]).wait()

    for key in moves:
        copy_of(key).wait_send()
    for i in (0, 1):
        q_copy(i).wait_send()
    piece = ctx.at[0, pl.ds(0, ROWS)]
    for s in (0, 1):
        for dx in (1, 2, 3):
            out_copy(s, dx, piece, piece).wait_send()

        @pl.when(core != s)
        def _():
            out_copy(s, 0, piece, piece).wait_send()


COPIES = 192


def local(tokens, positions, w_query, w_key, w_value):
    anywhere = pl.BlockSpec(memory_space=pltpu.HBM)
    vmem = pl.BlockSpec(memory_space=pltpu.VMEM)
    return pl.pallas_call(
        kernel_body,
        name="layer",
        out_shape=jax.ShapeDtypeStruct((ROWS, 2048), jnp.bfloat16),
        in_specs=[anywhere, vmem, anywhere, anywhere, anywhere],
        out_specs=vmem,
        scratch_shapes=[
            pltpu.VMEM((NX, NY, ROWS, 2048), jnp.bfloat16),
            pltpu.VMEM((2, NZ * NX, 256, 256), jnp.bfloat16),
            pltpu.VMEM((8192, 4 * HD), jnp.bfloat16),
            pltpu.VMEM((ROWS, 4 * HD), jnp.float32),
            pltpu.VMEM((2, ROWS, 2 * HD), jnp.bfloat16),
            pltpu.VMEM((2 * NZ, CHUNK, 2 * HD), jnp.bfloat16),
            pltpu.VMEM((2 * NZ, CHUNK, HD), jnp.bfloat16),
            pltpu.VMEM((2, 2, CHUNK, 2 * HD), jnp.bfloat16),
            pltpu.VMEM((CHUNK, 256), jnp.bfloat16),
            pltpu.VMEM((CHUNK, 256), jnp.bfloat16),
            pltpu.VMEM((CHUNK, 256), jnp.float32),
            pltpu.VMEM((64, HD), jnp.float32),
            pltpu.VMEM((2, 2, CHUNK, HD), jnp.float32),
            pltpu.VMEM((2, 2, CHUNK, 2 * HD), jnp.float32),
            pltpu.VMEM((2, CHUNK, 256), jnp.bfloat16),
            pltpu.SemaphoreType.DMA((6,)),
            pltpu.SemaphoreType.DMA((COPIES,)),
            pltpu.SemaphoreType.DMA((COPIES,)),
            pltpu.SemaphoreType.DMA((2, 2)),
            pltpu.SemaphoreType.DMA((2, 4)),
            pltpu.SemaphoreType.DMA((8,)),
        ],
        compiler_params=pltpu.CompilerParams(
            collective_id=0, has_side_effects=True, vmem_limit_bytes=60 * 2**20),
    )(tokens, positions.reshape(64, HD), w_query, w_key, w_value)


def solution(mesh):
    in_specs = (P(("seq", "row"), "col"), P(), P("row", "col"), P(None, "col"), P(None, "col"))
    out_specs = P(("seq", "row"), "col")
    return jax.shard_map(local, mesh=mesh, in_specs=in_specs, out_specs=out_specs, check_vma=False)
```

```python
import functools
import math

import jax
import jax.numpy as jnp
from jax import lax
from jax.experimental import pallas as pl
from jax.experimental.pallas import tpu as pltpu
from jax.sharding import PartitionSpec as P

HD = 128
NX, NY, NZ = 4, 4, 8
ROWS = 128
CHUNK = NX * ROWS
MESH = pl.DeviceIdType.MESH
LOG2E = 1.4426950408889634
NEG = -1e30
CUT = (1, 1, 2)
ORDER = (0, 1, 3, 2)


def place():
    row = lax.axis_index("row")
    return lax.axis_index("seq"), row // NX, row % NX, lax.axis_index("col")


def greet(partners):
    barrier = pltpu.get_barrier_semaphore()
    for partner in partners:
        pl.semaphore_signal(barrier, inc=1, device_id=partner, device_id_type=MESH)
    pl.semaphore_wait(barrier, len(partners))

DEFER = (True, True)

PLAN = (
    "feat", ("w", 1), ("w", 3), ("W", 1, 1, 0), ("W", -1, 1, 0), ("t", 0, 0, 1, 0, 0, -1),
    ("t", 0, 0, -1, 0, 0, -1), ("w", 2), ("W", 1, 1, 2), ("W", -1, 1, 2), ("W", 1, 1, 1),
    ("W", -1, 1, 1), ("t", 1, 1, 1, 0, 0, -1), ("t", 1, 1, -1, 0, 0, -1),
    ("t", 1, 0, 1, 0, 0, -1), ("t", 1, 0, -1, 0, 0, -1), ("W", 1, 2, 0), ("W", -1, 2, 0),
    ("t", 0, 0, 1, 0, -1, 0), ("t", 0, 0, -1, 0, 1, 1), ("W", 1, 1, 3), ("W", -1, 1, 3),
    ("t", 0, 1, 1, 0, 0, -1), ("t", 0, 1, -1, 0, 0, -1), ("W", 1, 2, 2), ("W", -1, 2, 2), "kv",
    ("t", 0, 1, 1, 0, -1, -1), ("t", 0, 1, -1, 0, -1, -1), ("W", 1, 2, 1), ("W", -1, 2, 1),
    ("t", 1, 1, -1, 0, -1, -1), ("t", 1, 1, 1, 0, -1, -1), ("W", 1, 3, 0), ("W", -1, 3, 0),
    ("t", 0, 1, 1, 0, 1, -1), ("t", 0, 1, -1, 0, 1, -1), ("W", 1, 2, 3), ("W", -1, 2, 3),
    ("t", 1, 0, -1, 0, 1, 1), ("t", 1, 1, -1, 0, 1, -1), ("t", 1, 1, 1, 0, 1, -1),
    ("t", 1, 0, 1, 0, -1, 0), ("W", 1, 3, 2), ("W", -1, 3, 2), ("t", 0, 1, 1, 0, -2, 0),
    ("W", 1, 3, 1), ("W", -1, 3, 1), ("t", 0, 1, -1, 0, 2, 1), ("W", 1, 4, 0), ("W", -1, 3, 3),
    ("t", 1, 1, -1, 0, 2, 1), ("kx", 1), ("kx", 3), ("W", 1, 3, 3), ("W", -1, 4, 2),
    ("W", 1, 4, 1), ("W", -1, 4, 3), ("kx", 2), ("K", 1, 1, 0), ("K", -1, 1, 0),
    ("t", 1, 1, 1, 0, -2, 0), ("K", 1, 1, 1), ("K", -1, 1, 1), "q01s", ("K", 1, 1, 2),
    ("K", -1, 1, 2), ("K", 1, 1, 3), ("K", -1, 1, 3), "q01c", ("K", 1, 2, 0), ("K", -1, 2, 0),
    ("K", 1, 2, 1), ("K", -1, 2, 1), "q2s", ("K", 1, 2, 2), ("K", -1, 2, 2),
)
LATE = (
    (("K", 1, 2, 3), ("K", -1, 2, 3), ("K", 1, 3, 0), ("K", -1, 3, 0), ),
    (("K", 1, 3, 1), ("K", -1, 3, 1), ("K", 1, 3, 2), ("K", -1, 3, 2), ("K", 1, 3, 3), ("K", -1, 3, 3), ),
    (("K", 1, 4, 0), ("K", 1, 4, 1), ("K", -1, 4, 2), ("K", -1, 4, 3), ),
    (),
)

COLUMNS = {(0, -1): (0, 896), (0, 0): (0, 384), (0, 1): (384, 512),
           (1, -1): (896, 1152), (1, 0): (896, 640), (1, 1): (1536, 512)}
FROM = {1: 3, 2: 1, 3: 2}


def token_moves():
    t = "t"
    moves = {}
    beside = [(t, 1, 1, s, 0, 0, -1) for s in (1, -1)]
    next_to = [(t, 1, 1, s, 0, b, -1) for s in (1, -1) for b in (1, -1)]
    for h in (0, 1):
        for s in (1, -1):
            moves[t, h, h, s, 0, 0, -1] = ()
    for h in (1, 0):
        for s in (1, -1):
            moves[t, h, 1 - h, s, 0, 0, -1] = ()
    for h in (0, 1):
        for s, p in ((1, 0), (-1, 1)):
            moves[t, h, 0, s, 0, -s, p] = ((t, h, 0, s, 0, 0, -1),)
        for s, p in ((1, 0), (-1, 1)):
            moves[t, h, 1, s, -s, 0, p] = ((t, h, 1, s, 0, 0, -1),)
        for s, p in ((1, 0), (-1, 1)):
            for s2 in (1, -1):
                moves[t, h, 1, s2, 0, -s, -1] = (
                    (t, h, 0, s, 0, 0, -1),) + tuple(beside if h and DEFER[0] else ())
        for s, p in ((1, 0), (-1, 1)):
            for b in (1, -1):
                moves[t, h, 1, s, -s, b, p] = ((t, h, 1, s, 0, b, -1),)
        for s, p in ((1, 0), (-1, 1)):
            for s2 in (1, -1):
                moves[t, h, 1, s2, 0, -2 * s, p] = (
                    (t, h, 0, s, 0, -s, p),) + tuple(next_to if h and DEFER[1] else ())
        for s, p in ((1, 0), (-1, 1)):
            moves[t, h, 1, s, -s, -2 * s, p] = ((t, h, 1, s, 0, -2 * s, p),)
    return moves


def ring_moves(name, first):
    moves = {}
    for r in range(4):
        for s in (1, -1):
            moves[name, s, 1, r] = first[r]
        moves[name + "c", 0, r] = first[r]
    for dist in (1, 2, 3, 4):
        for r in range(4):
            for s in (1, -1):
                if dist < 3 or (dist == 3 and s == (1 if r < 2 else -1)):
                    moves[name, s, dist + 1, r] = ((name, s, dist, r),)
                if dist < 4 or s == (1 if r < 2 else -1):
                    moves[name + "c", -s * dist, r] = ((name, s, dist, r),)
    return moves


def all_moves():
    moves = {("w", dx): () for dx in (1, 3, 2)}
    moves.update({("kx", dx): ("kv",) for dx in (1, 3, 2)})
    moves.update(token_moves())
    moves.update(ring_moves("W", [()] + [(("w", FROM[r]),) for r in (1, 2, 3)]))
    after = tuple(("W", s, 3, r) for s in (1, -1) for r in range(4))
    moves.update(ring_moves(
        "K", [("kv",) + after] + [(("kx", FROM[r]),) + after for r in (1, 2, 3)]))
    return moves


def kernel_body(
    tok_ref, pos_ref, wq_ref, wk_ref, wv_ref, out_ref, tok, wq, wkv, kvacc, kvown, kv, feat, q, qsend, qland, acc,
    docs, top, ctx_acc, ctx, loc, ssem, rsem,
    qsem, osend, orecv
):
    core, z, x, y = place()
    sib = 1 - core

    def at(dz=0, dx=0, dy=0, c=core):
        return (c, (z + dz) % NZ * NX + (x + dx) % NX, (y + dy) % NY)

    moves = all_moves()
    slots = {key: i for i, key in enumerate(moves)}
    done, sent = set(), set()

    def block(h, a, b, part):
        u, v = (a, b) if h == 0 else (b, a)
        start, size = COLUMNS[h, part]
        return tok.at[(x + u) % NX, (y + v) % NY, :, pl.ds(start, size)]

    def w_unit(dz, r, c=core):
        return wq.at[c, (z + dz) % NZ * NX + (x + ORDER[r]) % NX]

    def kv_unit(dz, r, c=core):
        return kv.at[c * NZ + (z + dz) % NZ, pl.ds(r * ROWS, ROWS)]

    def ends(key):
        kind = key[0]
        if kind == "t":
            _, h, order, s, a, b, part = key
            src = block(h, a, b, part)
            land = block(h, a, b - s, part) if order == 0 else block(h, a - s, b, part)
            return src, src, at(dy=s) if h == order else at(dx=s), land
        if kind == "w":
            dx = key[1]
            cols = pl.ds(pl.multiple_of((x + dx) % NX * 512 + core * 256, 256), 256)
            return wq_ref.at[:, cols], w_unit(0, 0), at(dx=dx), w_unit(0, ORDER.index(NX - dx))
        if kind == "kx":
            dx = key[1]
            land = kv_unit(0, ORDER.index(NX - dx))
            return kvown.at[(x + dx) % NX // 2], land, at(dx=dx), land
        unit = w_unit if kind[0] == "W" else kv_unit
        if kind[1:] == "c":
            src = unit(key[1], key[2])
            return src, src, at(c=sib), unit(key[1], key[2], sib)
        _, s, dist, r = key
        src = unit(-s * (dist - 1), r)
        return src, src, at(dz=s), unit(-s * dist, r)

    def copy_of(key):
        src, dst, device, _ = ends(key)
        i = slots[key]
        return pltpu.make_async_remote_copy(
            src_ref=src, dst_ref=dst, send_sem=ssem.at[i], recv_sem=rsem.at[i],
            device_id=device, device_id_type=MESH)

    def fire():
        for key, needs in moves.items():
            if key not in sent and all(need in done for need in needs):
                sent.add(key)
                copy_of(key).start()

    def take(key):
        if key in done:
            return
        land = ends(key)[3]
        i = slots[key]
        pltpu.make_async_remote_copy(
            src_ref=land, dst_ref=land, send_sem=ssem.at[i], recv_sem=rsem.at[i],
            device_id=at(c=sib), device_id_type=MESH).wait_recv()
        done.add(key)
        fire()

    def take_tokens(offsets):
        for key in moves:
            if key[0] == "t":
                _, h, order, s, a, b, _ = key
                a, b = (a, b - s) if order == 0 else (a - s, b)
                if (a if h == 0 else b) % NX in offsets:
                    take(key)

    def document_features():
        first = (pos_ref[...] == 0).astype(jnp.bfloat16)
        r = lax.broadcasted_iota(jnp.int32, (HD, HD), 0)
        c = lax.broadcasted_iota(jnp.int32, (HD, HD), 1)
        within = jnp.dot(first, (r <= c).astype(jnp.bfloat16), preferred_element_type=jnp.float32)
        total = jnp.broadcast_to(within[:, HD - 1:], within.shape).astype(jnp.bfloat16)
        before = (c < r).astype(jnp.bfloat16)[:64, :64]
        docs[...] = within + jnp.dot(before, total, preferred_element_type=jnp.float32)

        def body(b, carry):
            for part in range(CHUNK // HD):
                row = docs[pl.ds(b * NX + (x + ORDER[part]) % NX, 1), :]
                hot = jnp.broadcast_to(row, (HD, HD)) == r.astype(jnp.float32)
                feat[pl.ds(b, 1), part * HD:(part + 1) * HD, :] = (
                    hot.astype(jnp.float32).T.astype(jnp.bfloat16).reshape(1, HD, HD))
            return carry

        lax.fori_loop(0, 2 * NZ, body, 0)
        for s in range(2):
            hot = feat[pl.ds(s * NZ + z, 1)].reshape(CHUNK, HD).astype(jnp.float32)
            bar = ((1.0 - hot) * NEG).astype(jnp.bfloat16)
            for g in range(2):
                q[s, g, :, HD:] = bar

    my_w = pl.ds(pl.multiple_of(x * 512 + core * 256, 256), 256)
    loads = [
        pltpu.make_async_copy(tok_ref, tok.at[x, y], loc.at[0]),
        pltpu.make_async_copy(wq_ref.at[:, my_w], wq.at[core, z * NX + x], loc.at[1]),
    ]
    for i in range(4):
        source = (wk_ref, wv_ref)[i % 2].at[:, pl.ds(i // 2 * HD, HD)]
        loads.append(pltpu.make_async_copy(source, wkv.at[:, pl.ds(i * HD, HD)], loc.at[2 + i]))
    for load in loads:
        load.start()

    greet([at(dx=1), at(dx=2), at(dx=3), at(dy=1), at(dy=3), at(dz=1), at(dz=7), at(c=sib),
           at(dx=1, c=sib), at(dx=2, c=sib), at(dx=3, c=sib)])

    loads[0].wait()
    loads[1].wait()
    fire()

    def tokens_of(dxs, yy):
        return jnp.concatenate(
            [tok[pl.ds((x + dx) % NX, 1), pl.ds(yy, 1)].reshape(ROWS, 2048) for dx in dxs], axis=0)

    def kv_project():
        kvacc[...] = jnp.zeros_like(kvacc)

        def body(j, carry):
            kvacc[...] += jnp.dot(
                tokens_of((0,), j), wkv[pl.ds(pl.multiple_of(j * 2048, 2048), 2048), :],
                preferred_element_type=jnp.float32)
            return carry

        lax.fori_loop(0, NY, body, 0)
        for head in (0, 1):
            kvown[head] = kvacc[:, head * 256:head * 256 + 256].astype(jnp.bfloat16)
        kv[pl.ds(core * NZ + z, 1), 0:ROWS] = kvown[pl.ds(x // 2, 1)]

    def q_copy(i):
        rows = pl.ds((0, 384)[i], (384, 128)[i])
        return pltpu.make_async_remote_copy(
            src_ref=qsend.at[rows], dst_ref=qland.at[rows], send_sem=qsem.at[0, i],
            recv_sem=qsem.at[1, i], device_id=at(c=sib), device_id_type=MESH)

    def q_project(dxs, first, cores):
        size = len(dxs) * ROWS
        rows, width = pl.ds(first, size), pl.ds(0, 256 * len(cores))
        acc[rows, width] = jnp.zeros((size, 256 * len(cores)), jnp.float32)

        def body(j, carry):
            weights = [wq[pl.ds(c, 1), pl.ds(j * 8, 8)].reshape(2048, 256) for c in cores]
            acc[rows, width] += jnp.dot(
                tokens_of(dxs, j), jnp.concatenate(weights, axis=1),
                preferred_element_type=jnp.float32)
            return carry

        lax.fori_loop(0, NY, body, 0)

        def columns(c):
            start = pl.multiple_of(c * 256, 256) if len(cores) == 2 else 0
            found = acc[rows, pl.ds(start, 256)]
            return (found * (LOG2E / math.sqrt(HD))).astype(jnp.bfloat16)

        if len(cores) == 2 or cores[0] is sib:
            qsend[rows, :] = columns(sib)
            q_copy(0 if first == 0 else 1).start()
        if len(cores) == 2 or cores[0] is core:
            found = columns(core)
            for g in (0, 1):
                q[pl.ds(core, 1), g, rows, :HD] = found[:, g * HD:(g + 1) * HD].reshape(
                    1, size, HD)

    def kv_core_wait(dist):
        for key in moves:
            if key[0] == "Kc" and abs(key[1]) == dist:
                take(key)

    for entry in PLAN:
        if entry == "feat":
            document_features()
        elif entry == "kv":
            take_tokens((0,))
            for load in loads[2:]:
                load.wait()
            kv_project()
            done.add("kv")
            fire()
        elif entry == "q01s":
            take_tokens((0, 1, 3))
            for key in moves:
                if key[0][0] == "W":
                    take(key)
            q_project((0, 1, 3), 0, (sib,))
        elif entry == "q01c":
            q_project((0, 1, 3), 0, (core,))
        elif entry == "q2s":
            take_tokens((2,))
            q_project((2,), 384, (0, 1))
        else:
            take(entry)
    for i in (0, 1):
        q_copy(i).wait_recv()
    for g in (0, 1):
        q[pl.ds(sib, 1), g, :, :HD] = qland[:, g * HD:(g + 1) * HD].reshape(1, CHUNK, HD)
    kv_core_wait(0)

    def places(dim):
        size = (HD, CHUNK) if dim == 0 else (CHUNK, HD)
        return jnp.concatenate(
            [lax.broadcasted_iota(jnp.int32, size, dim) + (x + dx) % NX * ROWS for dx in ORDER],
            axis=dim)

    def scores_of(piece):
        s, g, blocks, rows = piece
        queries = q[s, g, rows, :]
        found = []
        for b, diagonal in blocks:
            keys = jnp.concatenate(
                [kv[pl.ds(b, 1), :, :HD], feat[pl.ds(b, 1)]], axis=2).reshape(CHUNK, 2 * HD)
            one = lax.dot_general(
                queries, keys, (((1,), (1,)), ((), ())), preferred_element_type=jnp.float32)
            if diagonal:
                one = jnp.where(places(1) <= places(0), one, NEG)
            found.append(one)
        return found

    def attend(pieces, fresh=False, cut=1):
        size = CHUNK // cut
        pieces = [p + (pl.ds(i * size, size),) for p in pieces for i in range(cut)]
        ahead = scores_of(pieces[0])
        for i, (s, g, blocks, rows) in enumerate(pieces):
            found = ahead
            if i + 1 < len(pieces):
                ahead = scores_of(pieces[i + 1])
            high = jnp.max(functools.reduce(jnp.maximum, found), axis=1, keepdims=True)
            high = jnp.broadcast_to(high, (size, HD))
            if not fresh:
                old = top[s, g, rows, :]
                high = jnp.maximum(old, high)
                shrink = jnp.exp2(old - high)
            top[s, g, rows, :] = high
            wide = jnp.concatenate([high] * (CHUNK // HD), axis=1)
            added = None
            for one, (b, _) in zip(found, blocks):
                weight = jnp.exp2(one - wide).astype(jnp.bfloat16)
                values = jnp.concatenate(
                    [kv[pl.ds(b, 1), :, HD:].reshape(CHUNK, HD),
                     jnp.ones((CHUNK, HD), jnp.bfloat16)], axis=1)
                part = jnp.dot(weight, values, preferred_element_type=jnp.float32)
                added = part if added is None else added + part
            if not fresh:
                added += ctx_acc[s, g, rows, :] * jnp.concatenate([shrink, shrink], axis=1)
            ctx_acc[s, g, rows, :] = added

    def finish(s):
        for g in (0, 1):
            ctx[s, :, g * HD:(g + 1) * HD] = (
                ctx_acc[s, g, :, :HD] / ctx_acc[s, g, :, HD:]).astype(jnp.bfloat16)
        cols = pl.ds(pl.multiple_of(x * 512 + core * 256, 256), 256)
        for r in (3, 1, 2, 0):
            src, dst = ctx.at[s, pl.ds(r * ROWS, ROWS)], out_ref.at[:, cols]
            if r:
                out_copy(s, ORDER[r], src, dst).start()
            else:
                @pl.when(core == s)
                def _():
                    pltpu.make_async_copy(src, dst, loc.at[0]).start()

                @pl.when(core != s)
                def _():
                    out_copy(s, 0, src, dst).start()

    def out_copy(s, dx, src, dst):
        return pltpu.make_async_remote_copy(
            src_ref=src, dst_ref=dst, send_sem=osend.at[s, dx], recv_sem=orecv.at[4 * core + dx],
            device_id=at(dx=dx, c=s), device_id_type=MESH)

    attend([(1, 0, [(z, False), (NZ + z, True)]), (1, 1, [(z, False), (NZ + z, True)]),
            (0, 0, [(z, True)]), (0, 1, [(z, True)])], fresh=True)

    @pl.when(z == 0)
    def _():
        finish(0)

    def kv_round(dist, carry):
        for now in (1, 2, 3):
            @pl.when(dist == now)
            def _():
                for key in LATE[now - 1]:
                    take(key)
                kv_core_wait(now)

        low, high = (z + NZ - dist) % NZ, (z + dist) % NZ
        both = [(low, False), (high, False)]
        count = jnp.where(low < z, 1, 0) + jnp.where(high < z, 1, 0)

        @pl.when(count == 0)
        def _():
            attend([(1, 0, both), (1, 1, both)], cut=CUT[0])

        @pl.when(count == 1)
        def _():
            one = jnp.where(low < z, low, high)
            three = both + [(NZ + one, False)]
            attend([(1, 0, three), (1, 1, three),
                    (0, 0, [(one, False)]), (0, 1, [(one, False)])], cut=CUT[1])

        @pl.when(count == 2)
        def _():
            four = both + [(NZ + low, False), (NZ + high, False)]
            attend([(1, 0, four), (1, 1, four), (0, 0, both), (0, 1, both)], cut=CUT[2])

        @pl.when(dist == z)
        def _():
            finish(0)

        return carry

    lax.fori_loop(1, 4, kv_round, 0)

    for key in LATE[3]:
        take(key)
    kv_core_wait(4)
    far = (z + 4) % NZ

    @pl.when(far < z)
    def _():
        attend([(0, 0, [(far, False)]), (0, 1, [(far, False)])])
        finish(0)
        two = [(far, False), (NZ + far, False)]
        attend([(1, 0, two), (1, 1, two)])

    @pl.when(far >= z)
    def _():
        attend([(1, 0, [(far, False)]), (1, 1, [(far, False)])])

    finish(1)

    def out_land(c, dx):
        return out_ref.at[:, pl.ds(pl.multiple_of((x - dx) % NX * 512 + c * 256, 256), 256)]

    def out_wait(c, dx):
        land = out_land(c, dx)
        pltpu.make_async_remote_copy(
            src_ref=land, dst_ref=land, send_sem=osend.at[0, dx], recv_sem=orecv.at[4 * c + dx],
            device_id=at(c=sib), device_id_type=MESH).wait_recv()

    for c in (0, 1):
        for dx in (1, 2, 3):
            out_wait(c, dx)
    out_wait(sib, 0)
    own = out_land(core, 0)
    pltpu.make_async_copy(own, own, loc.at[0]).wait()

    for key in moves:
        copy_of(key).wait_send()
    for i in (0, 1):
        q_copy(i).wait_send()
    piece = ctx.at[0, pl.ds(0, ROWS)]
    for s in (0, 1):
        for dx in (1, 2, 3):
            out_copy(s, dx, piece, piece).wait_send()

        @pl.when(core != s)
        def _():
            out_copy(s, 0, piece, piece).wait_send()


COPIES = 192


def local(tokens, positions, w_query, w_key, w_value):
    anywhere = pl.BlockSpec(memory_space=pltpu.HBM)
    vmem = pl.BlockSpec(memory_space=pltpu.VMEM)
    return pl.pallas_call(
        kernel_body,
        name="layer",
        out_shape=jax.ShapeDtypeStruct((ROWS, 2048), jnp.bfloat16),
        in_specs=[anywhere, vmem, anywhere, anywhere, anywhere],
        out_specs=vmem,
        scratch_shapes=[
            pltpu.VMEM((NX, NY, ROWS, 2048), jnp.bfloat16),
            pltpu.VMEM((2, NZ * NX, 256, 256), jnp.bfloat16),
            pltpu.VMEM((8192, 4 * HD), jnp.bfloat16),
            pltpu.VMEM((ROWS, 4 * HD), jnp.float32),
            pltpu.VMEM((2, ROWS, 2 * HD), jnp.bfloat16),
            pltpu.VMEM((2 * NZ, CHUNK, 2 * HD), jnp.bfloat16),
            pltpu.VMEM((2 * NZ, CHUNK, HD), jnp.bfloat16),
            pltpu.VMEM((2, 2, CHUNK, 2 * HD), jnp.bfloat16),
            pltpu.VMEM((CHUNK, 256), jnp.bfloat16),
            pltpu.VMEM((CHUNK, 256), jnp.bfloat16),
            pltpu.VMEM((CHUNK, 512), jnp.float32),
            pltpu.VMEM((64, HD), jnp.float32),
            pltpu.VMEM((2, 2, CHUNK, HD), jnp.float32),
            pltpu.VMEM((2, 2, CHUNK, 2 * HD), jnp.float32),
            pltpu.VMEM((2, CHUNK, 256), jnp.bfloat16),
            pltpu.SemaphoreType.DMA((6,)),
            pltpu.SemaphoreType.DMA((COPIES,)),
            pltpu.SemaphoreType.DMA((COPIES,)),
            pltpu.SemaphoreType.DMA((2, 2)),
            pltpu.SemaphoreType.DMA((2, 4)),
            pltpu.SemaphoreType.DMA((8,)),
        ],
        compiler_params=pltpu.CompilerParams(
            collective_id=0, has_side_effects=True, vmem_limit_bytes=60 * 2**20),
    )(tokens, positions.reshape(64, HD), w_query, w_key, w_value)


def solution(mesh):
    in_specs = (P(("seq", "row"), "col"), P(), P("row", "col"), P(None, "col"), P(None, "col"))
    out_specs = P(("seq", "row"), "col")
    return jax.shard_map(local, mesh=mesh, in_specs=in_specs, out_specs=out_specs, check_vma=False)
```

```python
import functools
import math

import jax
import jax.numpy as jnp
from jax import lax
from jax.experimental import pallas as pl
from jax.experimental.pallas import tpu as pltpu
from jax.sharding import PartitionSpec as P

HD = 128
NX, NY, NZ = 4, 4, 8
ROWS = 128
CHUNK = NX * ROWS
MESH = pl.DeviceIdType.MESH
LOG2E = 1.4426950408889634
NEG = -1e30
CUT = (1, 1, 2)
ORDER = (0, 1, 3, 2)


def place():
    row = lax.axis_index("row")
    return lax.axis_index("seq"), row // NX, row % NX, lax.axis_index("col")


def greet(partners):
    barrier = pltpu.get_barrier_semaphore()
    for partner in partners:
        pl.semaphore_signal(barrier, inc=1, device_id=partner, device_id_type=MESH)
    pl.semaphore_wait(barrier, len(partners))

DEFER = (True, True)

PLAN = (
    "feat", ("w", 1), ("w", 3), ("W", 1, 1, 0), ("W", -1, 1, 0), ("t", 0, 0, 1, 0, 0, -1),
    ("t", 0, 0, -1, 0, 0, -1), ("w", 2), ("W", 1, 1, 2), ("W", -1, 1, 2), ("W", 1, 1, 1),
    ("W", -1, 1, 1), ("t", 1, 1, 1, 0, 0, -1), ("t", 1, 1, -1, 0, 0, -1),
    ("t", 1, 0, 1, 0, 0, -1), ("t", 1, 0, -1, 0, 0, -1), ("W", 1, 2, 0), ("W", -1, 2, 0),
    ("t", 0, 0, 1, 0, -1, 0), ("t", 0, 0, -1, 0, 1, 1), ("W", 1, 1, 3), ("W", -1, 1, 3),
    ("t", 0, 1, 1, 0, 0, -1), ("t", 0, 1, -1, 0, 0, -1), ("W", 1, 2, 2), ("W", -1, 2, 2), "kv",
    ("t", 0, 1, 1, 0, -1, -1), ("t", 0, 1, -1, 0, -1, -1), ("W", 1, 2, 1), ("W", -1, 2, 1),
    ("t", 1, 1, -1, 0, -1, -1), ("t", 1, 1, 1, 0, -1, -1), ("t", 1, 0, -1, 0, 1, 1),
    ("W", 1, 3, 0), ("W", -1, 3, 0), ("t", 1, 0, 1, 0, -1, 0), ("t", 0, 1, 1, 0, -2, 0),
    ("W", 1, 2, 3), ("W", -1, 2, 3), ("t", 0, 1, -1, 0, 2, 1), ("t", 1, 1, -1, 0, 1, -1),
    ("t", 1, 1, 1, 0, 1, -1), ("W", 1, 3, 2), ("W", -1, 3, 2), ("W", 1, 3, 1), ("W", -1, 3, 1),
    ("kx", 1), ("kx", 3), ("W", 1, 4, 0), ("W", -1, 3, 3), ("kx", 2), ("W", 1, 3, 3),
    ("W", -1, 4, 2), ("t", 0, 1, 1, 0, 1, -1), ("t", 0, 1, -1, 0, 1, -1),
    ("t", 1, 1, 1, 0, -2, 0), "q01a", ("W", 1, 4, 1), ("W", -1, 4, 3), ("t", 1, 1, -1, 0, 2, 1),
    ("K", 1, 1, 0), ("K", -1, 1, 0), ("K", 1, 1, 1), ("K", -1, 1, 1), ("K", 1, 1, 2),
    ("K", -1, 1, 2), "q01b", ("K", 1, 1, 3), ("K", -1, 1, 3), ("K", 1, 2, 0), ("K", -1, 2, 0),
    "q2", ("K", 1, 2, 1), ("K", -1, 2, 1),
)
LATE = (
    (("K", 1, 2, 2), ("K", -1, 2, 2), ("K", 1, 2, 3), ("K", -1, 2, 3), ),
    (("K", 1, 3, 0), ("K", -1, 3, 0), ("K", 1, 3, 1), ("K", -1, 3, 1), ("K", 1, 3, 2), ("K", -1, 3, 2), ("K", 1, 3, 3), ("K", -1, 3, 3), ),
    (("K", 1, 4, 0), ("K", -1, 4, 2), ("K", 1, 4, 1), ("K", -1, 4, 3), ),
    (),
)

COLUMNS = {(0, -1): (0, 896), (0, 0): (0, 384), (0, 1): (384, 512),
           (1, -1): (896, 1152), (1, 0): (896, 640), (1, 1): (1536, 512)}
FROM = {1: 3, 2: 1, 3: 2}


def token_moves():
    t = "t"
    moves = {}
    beside = [(t, 1, 1, s, 0, 0, -1) for s in (1, -1)]
    next_to = [(t, 1, 1, s, 0, b, -1) for s in (1, -1) for b in (1, -1)]
    for h in (0, 1):
        for s in (1, -1):
            moves[t, h, h, s, 0, 0, -1] = ()
    for h in (1, 0):
        for s in (1, -1):
            moves[t, h, 1 - h, s, 0, 0, -1] = ()
    for h in (0, 1):
        for s, p in ((1, 0), (-1, 1)):
            moves[t, h, 0, s, 0, -s, p] = ((t, h, 0, s, 0, 0, -1),)
        for s, p in ((1, 0), (-1, 1)):
            moves[t, h, 1, s, -s, 0, p] = ((t, h, 1, s, 0, 0, -1),)
        for s, p in ((1, 0), (-1, 1)):
            for s2 in (1, -1):
                moves[t, h, 1, s2, 0, -s, -1] = (
                    (t, h, 0, s, 0, 0, -1),) + tuple(beside if h and DEFER[0] else ())
                if h == 0 and s == -1:
                    moves[t, h, 1, s2, 0, 1, -1] += ("kv",)
        for s, p in ((1, 0), (-1, 1)):
            for b in (1, -1):
                moves[t, h, 1, s, -s, b, p] = ((t, h, 1, s, 0, b, -1),)
        for s, p in ((1, 0), (-1, 1)):
            for s2 in (1, -1):
                moves[t, h, 1, s2, 0, -2 * s, p] = (
                    (t, h, 0, s, 0, -s, p),) + tuple(next_to if h and DEFER[1] else ())
        for s, p in ((1, 0), (-1, 1)):
            moves[t, h, 1, s, -s, -2 * s, p] = ((t, h, 1, s, 0, -2 * s, p),)
    return moves


def ring_moves(name, first):
    moves = {}
    for r in range(4):
        for s in (1, -1):
            moves[name, s, 1, r] = first[r]
        moves[name + "c", 0, r] = first[r]
    for dist in (1, 2, 3, 4):
        for r in range(4):
            for s in (1, -1):
                if dist < 3 or (dist == 3 and s == (1 if r < 2 else -1)):
                    moves[name, s, dist + 1, r] = ((name, s, dist, r),)
                if dist < 4 or s == (1 if r < 2 else -1):
                    moves[name + "c", -s * dist, r] = ((name, s, dist, r),)
    return moves


def all_moves():
    moves = {("w", dx): () for dx in (1, 3, 2)}
    moves.update({("kx", dx): ("kv",) for dx in (1, 3, 2)})
    moves.update(token_moves())
    moves.update(ring_moves("W", [()] + [(("w", FROM[r]),) for r in (1, 2, 3)]))
    after = tuple(("W", s, 3, r) for s in (1, -1) for r in range(4))
    moves.update(ring_moves(
        "K", [("kv",) + after] + [(("kx", FROM[r]),) + after for r in (1, 2, 3)]))
    return moves


def kernel_body(
    tok_ref, pos_ref, wq_ref, wk_ref, wv_ref, out_ref, tok, wq, wkv, kvacc, kvown, kv, feat, q, qsend, qland, acc,
    docs, top, ctx_acc, ctx, loc, ssem, rsem,
    qsem, osend, orecv
):
    core, z, x, y = place()
    sib = 1 - core

    def at(dz=0, dx=0, dy=0, c=core):
        return (c, (z + dz) % NZ * NX + (x + dx) % NX, (y + dy) % NY)

    moves = all_moves()
    slots = {key: i for i, key in enumerate(moves)}
    done, sent = set(), set()

    def block(h, a, b, part):
        u, v = (a, b) if h == 0 else (b, a)
        start, size = COLUMNS[h, part]
        return tok.at[(x + u) % NX, (y + v) % NY, :, pl.ds(start, size)]

    def w_unit(dz, r, c=core):
        return wq.at[c, (z + dz) % NZ * NX + (x + ORDER[r]) % NX]

    def kv_unit(dz, r, c=core):
        return kv.at[c * NZ + (z + dz) % NZ, pl.ds(r * ROWS, ROWS)]

    def ends(key):
        kind = key[0]
        if kind == "t":
            _, h, order, s, a, b, part = key
            src = block(h, a, b, part)
            land = block(h, a, b - s, part) if order == 0 else block(h, a - s, b, part)
            return src, src, at(dy=s) if h == order else at(dx=s), land
        if kind == "w":
            dx = key[1]
            cols = pl.ds(pl.multiple_of((x + dx) % NX * 512 + core * 256, 256), 256)
            return wq_ref.at[:, cols], w_unit(0, 0), at(dx=dx), w_unit(0, ORDER.index(NX - dx))
        if kind == "kx":
            dx = key[1]
            land = kv_unit(0, ORDER.index(NX - dx))
            return kvown.at[(x + dx) % NX // 2], land, at(dx=dx), land
        unit = w_unit if kind[0] == "W" else kv_unit
        if kind[1:] == "c":
            src = unit(key[1], key[2])
            return src, src, at(c=sib), unit(key[1], key[2], sib)
        _, s, dist, r = key
        src = unit(-s * (dist - 1), r)
        return src, src, at(dz=s), unit(-s * dist, r)

    def copy_of(key):
        src, dst, device, _ = ends(key)
        i = slots[key]
        return pltpu.make_async_remote_copy(
            src_ref=src, dst_ref=dst, send_sem=ssem.at[i], recv_sem=rsem.at[i],
            device_id=device, device_id_type=MESH)

    def fire():
        for key, needs in moves.items():
            if key not in sent and all(need in done for need in needs):
                sent.add(key)
                copy_of(key).start()

    def take(key):
        if key in done:
            return
        land = ends(key)[3]
        i = slots[key]
        pltpu.make_async_remote_copy(
            src_ref=land, dst_ref=land, send_sem=ssem.at[i], recv_sem=rsem.at[i],
            device_id=at(c=sib), device_id_type=MESH).wait_recv()
        done.add(key)
        fire()

    def take_tokens(offsets):
        for key in moves:
            if key[0] == "t":
                _, h, order, s, a, b, _ = key
                a, b = (a, b - s) if order == 0 else (a - s, b)
                if (a if h == 0 else b) % NX in offsets:
                    take(key)

    def document_features():
        first = (pos_ref[...] == 0).astype(jnp.bfloat16)
        r = lax.broadcasted_iota(jnp.int32, (HD, HD), 0)
        c = lax.broadcasted_iota(jnp.int32, (HD, HD), 1)
        within = jnp.dot(first, (r <= c).astype(jnp.bfloat16), preferred_element_type=jnp.float32)
        total = jnp.broadcast_to(within[:, HD - 1:], within.shape).astype(jnp.bfloat16)
        before = (c < r).astype(jnp.bfloat16)[:64, :64]
        docs[...] = within + jnp.dot(before, total, preferred_element_type=jnp.float32)

        def body(b, carry):
            for part in range(CHUNK // HD):
                row = docs[pl.ds(b * NX + (x + ORDER[part]) % NX, 1), :]
                hot = jnp.broadcast_to(row, (HD, HD)) == r.astype(jnp.float32)
                feat[pl.ds(b, 1), part * HD:(part + 1) * HD, :] = (
                    hot.astype(jnp.float32).T.astype(jnp.bfloat16).reshape(1, HD, HD))
            return carry

        lax.fori_loop(0, 2 * NZ, body, 0)
        for s in range(2):
            hot = feat[pl.ds(s * NZ + z, 1)].reshape(CHUNK, HD).astype(jnp.float32)
            bar = ((1.0 - hot) * NEG).astype(jnp.bfloat16)
            for g in range(2):
                q[s, g, :, HD:] = bar

    my_w = pl.ds(pl.multiple_of(x * 512 + core * 256, 256), 256)
    loads = [
        pltpu.make_async_copy(tok_ref, tok.at[x, y], loc.at[0]),
        pltpu.make_async_copy(wq_ref.at[:, my_w], wq.at[core, z * NX + x], loc.at[1]),
    ]
    for i in range(4):
        source = (wk_ref, wv_ref)[i % 2].at[:, pl.ds(i // 2 * HD, HD)]
        loads.append(pltpu.make_async_copy(source, wkv.at[:, pl.ds(i * HD, HD)], loc.at[2 + i]))
    for load in loads:
        load.start()

    greet([at(dx=1), at(dx=2), at(dx=3), at(dy=1), at(dy=3), at(dz=1), at(dz=7), at(c=sib),
           at(dx=1, c=sib), at(dx=2, c=sib), at(dx=3, c=sib)])

    loads[0].wait()
    loads[1].wait()
    fire()

    def tokens_of(dxs, yy):
        return jnp.concatenate(
            [tok[pl.ds((x + dx) % NX, 1), pl.ds(yy, 1)].reshape(ROWS, 2048) for dx in dxs], axis=0)

    def kv_project():
        kvacc[...] = jnp.zeros_like(kvacc)

        def body(j, carry):
            kvacc[...] += jnp.dot(
                tokens_of((0,), j), wkv[pl.ds(pl.multiple_of(j * 2048, 2048), 2048), :],
                preferred_element_type=jnp.float32)
            return carry

        lax.fori_loop(0, NY, body, 0)
        for head in (0, 1):
            kvown[head] = kvacc[:, head * 256:head * 256 + 256].astype(jnp.bfloat16)
        kv[pl.ds(core * NZ + z, 1), 0:ROWS] = kvown[pl.ds(x // 2, 1)]

    def q_copy(i):
        rows = pl.ds((0, 384)[i], (384, 128)[i])
        return pltpu.make_async_remote_copy(
            src_ref=qsend.at[rows], dst_ref=qland.at[rows], send_sem=qsem.at[0, i],
            recv_sem=qsem.at[1, i], device_id=at(c=sib), device_id_type=MESH)

    def q_add(dxs, first, count, start):
        rows = pl.ds(first, len(dxs) * ROWS)
        after = (z + 4) % NZ // 2 + 1 + start

        def body(j, carry):
            yy = (after + j) % NY
            weights = [wq[c, pl.ds(yy * 8, 8)].reshape(2048, 256) for c in (0, 1)]
            acc[rows, :] += jnp.dot(
                tokens_of(dxs, yy), jnp.concatenate(weights, axis=1),
                preferred_element_type=jnp.float32)
            return carry

        lax.fori_loop(0, count, body, 0)

    def q_finish(first, size):
        rows = pl.ds(first, size)

        def columns(c):
            found = acc[rows, pl.ds(pl.multiple_of(c * 256, 256), 256)]
            return (found * (LOG2E / math.sqrt(HD))).astype(jnp.bfloat16)

        qsend[rows, :] = columns(sib)
        q_copy(0 if first == 0 else 1).start()
        found = columns(core)
        for g in (0, 1):
            q[pl.ds(core, 1), g, rows, :HD] = found[:, g * HD:(g + 1) * HD].reshape(1, size, HD)

    def kv_core_wait(dist):
        for key in moves:
            if key[0] == "Kc" and abs(key[1]) == dist:
                take(key)

    for entry in PLAN:
        if entry == "feat":
            document_features()
        elif entry == "kv":
            take_tokens((0,))
            for load in loads[2:]:
                load.wait()
            kv_project()
            done.add("kv")
            fire()
        elif entry == "q01a":
            take_tokens((0, 1, 3))
            for key in moves:
                if key[0] == "W" and key[2] < 4 or key[0] == "Wc" and abs(key[1]) < 4:
                    take(key)
            acc[...] = jnp.zeros_like(acc)
            q_add((0, 1, 3), 0, NY - 1, 0)
        elif entry == "q01b":
            for key in moves:
                if key[0][0] == "W":
                    take(key)
            q_add((0, 1, 3), 0, 1, NY - 1)
            q_finish(0, 3 * ROWS)
        elif entry == "q2":
            take_tokens((2,))
            q_add((2,), 3 * ROWS, NY, 0)
            q_finish(3 * ROWS, ROWS)
        else:
            take(entry)
    for i in (0, 1):
        q_copy(i).wait_recv()
    for g in (0, 1):
        q[pl.ds(sib, 1), g, :, :HD] = qland[:, g * HD:(g + 1) * HD].reshape(1, CHUNK, HD)
    kv_core_wait(0)

    def places(dim):
        size = (HD, CHUNK) if dim == 0 else (CHUNK, HD)
        return jnp.concatenate(
            [lax.broadcasted_iota(jnp.int32, size, dim) + (x + dx) % NX * ROWS for dx in ORDER],
            axis=dim)

    def scores_of(piece):
        s, g, blocks, rows = piece
        queries = q[s, g, rows, :]
        found = []
        for b, diagonal in blocks:
            keys = jnp.concatenate(
                [kv[pl.ds(b, 1), :, :HD], feat[pl.ds(b, 1)]], axis=2).reshape(CHUNK, 2 * HD)
            one = lax.dot_general(
                queries, keys, (((1,), (1,)), ((), ())), preferred_element_type=jnp.float32)
            if diagonal:
                one = jnp.where(places(1) <= places(0), one, NEG)
            found.append(one)
        return found

    def attend(pieces, fresh=False, cut=1):
        size = CHUNK // cut
        pieces = [p + (pl.ds(i * size, size),) for p in pieces for i in range(cut)]
        ahead = scores_of(pieces[0])
        for i, (s, g, blocks, rows) in enumerate(pieces):
            found = ahead
            if i + 1 < len(pieces):
                ahead = scores_of(pieces[i + 1])
            high = jnp.max(functools.reduce(jnp.maximum, found), axis=1, keepdims=True)
            high = jnp.broadcast_to(high, (size, HD))
            if not fresh:
                old = top[s, g, rows, :]
                high = jnp.maximum(old, high)
                shrink = jnp.exp2(old - high)
            top[s, g, rows, :] = high
            wide = jnp.concatenate([high] * (CHUNK // HD), axis=1)
            added = None
            for one, (b, _) in zip(found, blocks):
                weight = jnp.exp2(one - wide).astype(jnp.bfloat16)
                values = jnp.concatenate(
                    [kv[pl.ds(b, 1), :, HD:].reshape(CHUNK, HD),
                     jnp.ones((CHUNK, HD), jnp.bfloat16)], axis=1)
                part = jnp.dot(weight, values, preferred_element_type=jnp.float32)
                added = part if added is None else added + part
            if not fresh:
                added += ctx_acc[s, g, rows, :] * jnp.concatenate([shrink, shrink], axis=1)
            ctx_acc[s, g, rows, :] = added

    def finish(s):
        for g in (0, 1):
            ctx[s, :, g * HD:(g + 1) * HD] = (
                ctx_acc[s, g, :, :HD] / ctx_acc[s, g, :, HD:]).astype(jnp.bfloat16)
        cols = pl.ds(pl.multiple_of(x * 512 + core * 256, 256), 256)
        for r in (3, 1, 2, 0):
            src, dst = ctx.at[s, pl.ds(r * ROWS, ROWS)], out_ref.at[:, cols]
            if r:
                out_copy(s, ORDER[r], src, dst).start()
            else:
                @pl.when(core == s)
                def _():
                    pltpu.make_async_copy(src, dst, loc.at[0]).start()

                @pl.when(core != s)
                def _():
                    out_copy(s, 0, src, dst).start()

    def out_copy(s, dx, src, dst):
        return pltpu.make_async_remote_copy(
            src_ref=src, dst_ref=dst, send_sem=osend.at[s, dx], recv_sem=orecv.at[4 * core + dx],
            device_id=at(dx=dx, c=s), device_id_type=MESH)

    attend([(1, 0, [(z, False), (NZ + z, True)]), (1, 1, [(z, False), (NZ + z, True)]),
            (0, 0, [(z, True)]), (0, 1, [(z, True)])], fresh=True)

    @pl.when(z == 0)
    def _():
        finish(0)

    def kv_round(dist, carry):
        for now in (1, 2, 3):
            @pl.when(dist == now)
            def _():
                for key in LATE[now - 1]:
                    take(key)
                kv_core_wait(now)

        low, high = (z + NZ - dist) % NZ, (z + dist) % NZ
        both = [(low, False), (high, False)]
        count = jnp.where(low < z, 1, 0) + jnp.where(high < z, 1, 0)

        @pl.when(count == 0)
        def _():
            attend([(1, 0, both), (1, 1, both)], cut=CUT[0])

        @pl.when(count == 1)
        def _():
            one = jnp.where(low < z, low, high)
            three = both + [(NZ + one, False)]
            attend([(1, 0, three), (1, 1, three),
                    (0, 0, [(one, False)]), (0, 1, [(one, False)])], cut=CUT[1])

        @pl.when(count == 2)
        def _():
            four = both + [(NZ + low, False), (NZ + high, False)]
            attend([(1, 0, four), (1, 1, four), (0, 0, both), (0, 1, both)], cut=CUT[2])

        @pl.when(dist == z)
        def _():
            finish(0)

        return carry

    lax.fori_loop(1, 4, kv_round, 0)

    for key in LATE[3]:
        take(key)
    kv_core_wait(4)
    far = (z + 4) % NZ

    @pl.when(far < z)
    def _():
        attend([(0, 0, [(far, False)]), (0, 1, [(far, False)])])
        finish(0)
        two = [(far, False), (NZ + far, False)]
        attend([(1, 0, two), (1, 1, two)])

    @pl.when(far >= z)
    def _():
        attend([(1, 0, [(far, False)]), (1, 1, [(far, False)])])

    finish(1)

    def out_land(c, dx):
        return out_ref.at[:, pl.ds(pl.multiple_of((x - dx) % NX * 512 + c * 256, 256), 256)]

    def out_wait(c, dx):
        land = out_land(c, dx)
        pltpu.make_async_remote_copy(
            src_ref=land, dst_ref=land, send_sem=osend.at[0, dx], recv_sem=orecv.at[4 * c + dx],
            device_id=at(c=sib), device_id_type=MESH).wait_recv()

    for c in (0, 1):
        for dx in (1, 2, 3):
            out_wait(c, dx)
    out_wait(sib, 0)
    own = out_land(core, 0)
    pltpu.make_async_copy(own, own, loc.at[0]).wait()

    for key in moves:
        copy_of(key).wait_send()
    for i in (0, 1):
        q_copy(i).wait_send()
    piece = ctx.at[0, pl.ds(0, ROWS)]
    for s in (0, 1):
        for dx in (1, 2, 3):
            out_copy(s, dx, piece, piece).wait_send()

        @pl.when(core != s)
        def _():
            out_copy(s, 0, piece, piece).wait_send()


COPIES = 192


def local(tokens, positions, w_query, w_key, w_value):
    anywhere = pl.BlockSpec(memory_space=pltpu.HBM)
    vmem = pl.BlockSpec(memory_space=pltpu.VMEM)
    return pl.pallas_call(
        kernel_body,
        name="layer",
        out_shape=jax.ShapeDtypeStruct((ROWS, 2048), jnp.bfloat16),
        in_specs=[anywhere, vmem, anywhere, anywhere, anywhere],
        out_specs=vmem,
        scratch_shapes=[
            pltpu.VMEM((NX, NY, ROWS, 2048), jnp.bfloat16),
            pltpu.VMEM((2, NZ * NX, 256, 256), jnp.bfloat16),
            pltpu.VMEM((8192, 4 * HD), jnp.bfloat16),
            pltpu.VMEM((ROWS, 4 * HD), jnp.float32),
            pltpu.VMEM((2, ROWS, 2 * HD), jnp.bfloat16),
            pltpu.VMEM((2 * NZ, CHUNK, 2 * HD), jnp.bfloat16),
            pltpu.VMEM((2 * NZ, CHUNK, HD), jnp.bfloat16),
            pltpu.VMEM((2, 2, CHUNK, 2 * HD), jnp.bfloat16),
            pltpu.VMEM((CHUNK, 256), jnp.bfloat16),
            pltpu.VMEM((CHUNK, 256), jnp.bfloat16),
            pltpu.VMEM((CHUNK, 512), jnp.float32),
            pltpu.VMEM((64, HD), jnp.float32),
            pltpu.VMEM((2, 2, CHUNK, HD), jnp.float32),
            pltpu.VMEM((2, 2, CHUNK, 2 * HD), jnp.float32),
            pltpu.VMEM((2, CHUNK, 256), jnp.bfloat16),
            pltpu.SemaphoreType.DMA((6,)),
            pltpu.SemaphoreType.DMA((COPIES,)),
            pltpu.SemaphoreType.DMA((COPIES,)),
            pltpu.SemaphoreType.DMA((2, 2)),
            pltpu.SemaphoreType.DMA((2, 4)),
            pltpu.SemaphoreType.DMA((8,)),
        ],
        compiler_params=pltpu.CompilerParams(
            collective_id=0, has_side_effects=True, vmem_limit_bytes=60 * 2**20),
    )(tokens, positions.reshape(64, HD), w_query, w_key, w_value)


def solution(mesh):
    in_specs = (P(("seq", "row"), "col"), P(), P("row", "col"), P(None, "col"), P(None, "col"))
    out_specs = P(("seq", "row"), "col")
    return jax.shard_map(local, mesh=mesh, in_specs=in_specs, out_specs=out_specs, check_vma=False)
```
